512 devices in a mesh: tp: 8 (over z_hi, core), dp: 64 (over x, y, z_lo).
Axes of the slice: x: 4, y: 4, z: 16 (z_hi: 4, z_lo: 4; z = z_hi * 4 + z_lo), core: 2. Of those that a mesh axis runs over, the one named last changes fastest.
Arguments:
- context: bfloat16 [16384, 4096], P('dp', 'tp'), may hold values from -6 to 6
- stream: bfloat16 [16384, 4096], P('dp'), may hold values from -16 to 16
- w_attn_out: bfloat16 [4096, 4096], P('tp', 'dp'), may hold values from -0.09375 to 0.09375
- modulation: float32 [64, 3, 4096], P('dp'), may hold values from -3 to 3
- w_teacher_head: bfloat16 [4096, 128], P('dp'), may hold values from -0.09375 to 0.09375
- noisy: bfloat16 [16384, 128], P('dp'), may hold values from -6 to 6
- timestep: int32 [64], P('dp'), may hold values from 0 to 999
- frames: int32 [64], P('dp'), may hold values from 1 to 256, as said below
- w_in: bfloat16 [128, 2048], replicated, may hold values from -0.5 to 0.5
- w_time: bfloat16 [128, 2048], replicated, may hold values from -0.5 to 0.5
- w_up: bfloat16 [2048, 3072], P('dp', 'tp'), may hold values from -0.125 to 0.125
- w_down: bfloat16 [3072, 2048], P('tp', 'dp'), may hold values from -0.109375 to 0.109375
- w_out: bfloat16 [2048, 128], P('dp'), may hold values from -0.125 to 0.125
Outputs:
- target: float32 [16384, 128], P('dp')
- loss: float32 [], replicated
- grad_up: float32 [2048, 3072], P('dp', 'tp')
The draws below stay inside these ranges and needn't reach their ends.
Inputs may be any that keep to these rules, and one draw needn't show every extreme that they name: The live frames of a clip are its first frames; some clip has all 256 live.
All inputs are finite; a program needn't handle non-finite values.
Results may differ from the reference program's by a relative error of at most 0.0085.
Values may be sent and summed in bfloat16 or wider, within the bound.
A program may use at most 64 MiB of HBM per device.

```python
import math
import jax
import jax.numpy as jnp
from jax import lax

D = 4096
C = 128
DS = 2048
FFS = 3072
FREQ = 128
STEPS = 1000
LEN = 256
CLIPS = 64
ROWS = 16384
N_TP = 8


def draw_stream(key, part):
    key = jax.random.fold_in(key, 7)
    key_base, key_cols = jax.random.split(key, 2)
    col_index = jnp.arange(D, dtype=jnp.float32)
    col_scale = jnp.exp(math.log(3.0) * col_index / D) * jax.random.uniform(key_cols, (D,), jnp.float32, 0.5, 1.5)
    base = jnp.clip(jax.random.normal(key_base, (ROWS, D), jnp.float32), -4.0, 4.0)
    return jnp.clip(base * col_scale[None, :], -16.0, 16.0).astype(jnp.bfloat16)


def draw_frames(key, part):
    key = jax.random.fold_in(key, 11)
    key_jitter, key_pick = jax.random.split(key, 2)
    clip_index = jnp.arange(CLIPS, dtype=jnp.int32)
    rising = LEN // 4 + 3 * LEN // 4 * clip_index // max(CLIPS - 1, 1)
    jitter = jax.random.randint(key_jitter, (CLIPS,), -(LEN // 8), LEN // 8 + 1, dtype=jnp.int32)
    values = jnp.clip(rising + jitter, 1, LEN)
    chosen = jax.random.randint(key_pick, (), 0, CLIPS, dtype=jnp.int32)
    return jnp.where(clip_index == chosen, LEN, values).astype(jnp.int32)


def place_ends(result, own_key, least, top_value):
    shape = result.shape
    spot = [jax.random.randint(jax.random.fold_in(own_key, axis), (), 0, shape[axis]) for axis in range(len(shape))]
    result = result.at[tuple(spot)].set(least)
    longest = shape.index(max(shape))
    spot[longest] = (spot[longest] + 1) % shape[longest]
    return result.at[tuple(spot)].set(top_value)


def block_scale(stream_key, shape, cuts, low, largest):
    factor_of, own = 1.0, jax.random.fold_in(stream_key, 6)
    for position, parts in cuts:
        draws = jnp.exp(jax.random.uniform(jax.random.fold_in(own, position), (parts,), jnp.float32, low / len(cuts), largest / len(cuts)))
        factor_of = factor_of * jnp.repeat(draws, shape[position] // parts).reshape([-1 if axis == position else 1 for axis in range(len(shape))])
    return factor_of


def gaussian(key, extent, scale, most, pieces=(), kind=jnp.bfloat16):
    result = scale * jax.random.normal(key, extent, jnp.float32)
    if pieces:
        result = result * block_scale(key, extent, pieces, -0.22, 0.18)
    return jnp.clip(result, -most, most).astype(kind)


def setup_inputs(seed: int = 0) -> dict:
    keys = jax.random.split(jax.random.key(seed), 14)
    context = gaussian(keys[0], (ROWS, D), 1.0, 6.0, ((0, 64), (1, 8)))
    stream = draw_stream(jax.random.fold_in(keys[13], 71), 0)
    w_attn_out = gaussian(keys[2], (D, D), D ** -0.5, 0.09375, ((0, 8), (1, 64)))
    modulation = gaussian(keys[3], (CLIPS, 3, D), 0.5, 3.0, ((0, 64),), jnp.float32)
    w_teacher_head = gaussian(keys[4], (D, C), D ** -0.5, 0.09375, ((0, 64),))
    noisy = gaussian(keys[5], (ROWS, C), 1.0, 6.0, ((0, 64),))
    timestep = place_ends(jax.random.randint(keys[6], (CLIPS,), 0, STEPS), jax.random.fold_in(keys[6], 1), 0, STEPS - 1).astype(jnp.int32)
    frames = draw_frames(jax.random.fold_in(keys[13], 71), 0)
    w_in = gaussian(keys[8], (C, DS), C ** -0.5, 0.5)
    w_time = gaussian(keys[9], (FREQ, DS), FREQ ** -0.5, 0.5)
    w_up = gaussian(keys[10], (DS, FFS), DS ** -0.5, 0.125, ((0, 64), (1, 8)))
    w_down = gaussian(keys[11], (FFS, DS), FFS ** -0.5, 0.109375, ((0, 8), (1, 64)))
    w_out = gaussian(keys[12], (DS, C), DS ** -0.5, 0.125, ((0, 64),))
    return dict(context=context, stream=stream, w_attn_out=w_attn_out, modulation=modulation, w_teacher_head=w_teacher_head, noisy=noisy, timestep=timestep, frames=frames, w_in=w_in, w_time=w_time, w_up=w_up, w_down=w_down, w_out=w_out)


loss_scale = 32768.0
norm_eps = 1e-06

def time_features(timestep):
    half = FREQ // 2
    freq_index = jnp.arange(half, dtype=jnp.float32)
    rates = jnp.exp(-math.log(10000.0) * freq_index / half)
    angles = timestep.astype(jnp.float32)[:, None] * rates[None, :]
    return jnp.concatenate([jnp.sin(angles), jnp.cos(angles)], axis=1).astype(jnp.bfloat16)

def noise_level(timestep):
    phase = (timestep.astype(jnp.float32) / STEPS + 0.008) / 1.008 * (math.pi / 2)
    return (jnp.cos(phase), jnp.sin(phase))

def gelu_slope(pre):
    inner_coef = math.sqrt(2.0 / math.pi)
    tangent = jnp.tanh(inner_coef * (pre + 0.044715 * pre * pre * pre))
    return 0.5 * (1.0 + tangent) + 0.5 * pre * (1.0 - tangent * tangent) * inner_coef * (1.0 + 3.0 * 0.044715 * pre * pre)

def blockwise_sum(left, right, blocks):
    width = left.shape[1] // blocks
    total = jnp.zeros((left.shape[0], right.shape[1]), jnp.float32)
    for block in range(blocks):
        part_prod = jnp.dot(left[:, block * width:(block + 1) * width], right[block * width:(block + 1) * width], preferred_element_type=jnp.float32)
        rounded = lax.optimization_barrier(part_prod.astype(jnp.bfloat16))
        total = total + rounded.astype(jnp.float32)
    return total

def reference(context, stream, w_attn_out, modulation, w_teacher_head, noisy, timestep, frames, w_in, w_time, w_up, w_down, w_out):
    attention = blockwise_sum(context, w_attn_out, N_TP).reshape(CLIPS, LEN, D)
    state = stream.astype(jnp.float32).reshape(CLIPS, LEN, D) + modulation[:, 0][:, None, :] * attention
    center = lax.optimization_barrier(jnp.mean(state, axis=-1, keepdims=True))
    spread = lax.optimization_barrier(jnp.mean((state - center) ** 2, axis=-1, keepdims=True))
    normed = (state - center) * lax.rsqrt(spread + norm_eps) * (1.0 + modulation[:, 2][:, None, :]) + modulation[:, 1][:, None, :]
    normed = normed.astype(jnp.bfloat16).reshape(ROWS, D)
    velocity = jnp.dot(normed, w_teacher_head, preferred_element_type=jnp.float32).reshape(CLIPS, LEN, C)
    signal, noise = noise_level(timestep)
    target = signal[:, None, None] * velocity + noise[:, None, None] * noisy.astype(jnp.float32).reshape(CLIPS, LEN, C)
    target = target.reshape(ROWS, C)
    features = time_features(timestep)
    time_rows = jnp.dot(features, w_time, preferred_element_type=jnp.float32)
    lifted_f = jnp.dot(noisy, w_in, preferred_element_type=jnp.float32).reshape(CLIPS, LEN, DS) + time_rows[:, None, :]
    lifted = jax.nn.silu(lifted_f).astype(jnp.bfloat16).reshape(ROWS, DS)
    pre = jnp.dot(lifted, w_up, preferred_element_type=jnp.float32)
    hidden = jax.nn.gelu(pre, approximate=True).astype(jnp.bfloat16)
    down = blockwise_sum(hidden, w_down, N_TP)
    mixed = lifted_f.reshape(ROWS, DS) + down
    inv_rms = lax.rsqrt(lax.optimization_barrier(jnp.mean(mixed * mixed, axis=-1, keepdims=True)) + norm_eps)
    unit = mixed * inv_rms
    pred = jnp.dot(unit.astype(jnp.bfloat16), w_out, preferred_element_type=jnp.float32)
    live = (jnp.arange(LEN, dtype=jnp.int32)[None, :] < frames[:, None]).astype(jnp.float32).reshape(ROWS, 1)
    count = jnp.sum(frames.astype(jnp.float32))
    error = pred - target
    loss = jnp.sum(live * error * error) / (count * C)
    grad_pred = (loss_scale * 2.0 / (count * C) * live * error).astype(jnp.bfloat16)
    grad_unit = jnp.dot(grad_pred, w_out.T, preferred_element_type=jnp.float32)
    grad_mixed = inv_rms * (grad_unit - unit * lax.optimization_barrier(jnp.mean(grad_unit * unit, axis=-1, keepdims=True)))
    grad_mixed = grad_mixed.astype(jnp.bfloat16)
    grad_hidden = jnp.dot(grad_mixed, w_down.T, preferred_element_type=jnp.float32)
    grad_pre = (grad_hidden * gelu_slope(pre)).astype(jnp.bfloat16)
    grad_up = jnp.dot(lifted.T, grad_pre, preferred_element_type=jnp.float32)
    return (target, loss, grad_up)
```

```python
import math

import jax
import jax.numpy as jnp
from jax import lax
from jax.experimental import pallas as pl
from jax.experimental.pallas import tpu as pltpu
from jax.sharding import PartitionSpec as P

C = 128
FREQ = 128
STEPS = 1000
LOSS_SCALE = 32768.0
EPS = 1e-06
F32 = jnp.float32
BF16 = jnp.bfloat16
MESH = pl.DeviceIdType.MESH
N_SEND = 520

COUNTS = dict(
    ctx=8, ag=128, ring=36, sib=32, sp=16, st=16, mod=16, head=4, nf=16, wo1=4, wo2=16, cnt=4,
    dn=16, un=32, tm=16, gp=16, lx=16, tg=8, lt=8, lz=4, g1=4, g2=4, g3=4, g4=16,
)
BASE = {}
N_RECV = 0
for _name, _count in COUNTS.items():
    BASE[_name] = N_RECV
    N_RECV += _count

XY = [(dx, dy) for dx in range(4) for dy in range(4) if dx or dy]


def dot_nt(a, b):
    return lax.dot_general(a, b, (((1,), (1,)), ((), ())), preferred_element_type=F32)


def dot_nn(a, b):
    return jnp.dot(a, b, preferred_element_type=F32)


def dot_tn(a, b):
    return lax.dot_general(a, b, (((0,), (0,)), ((), ())), preferred_element_type=F32)


def split_dot(a, b):
    high = a.astype(BF16)
    low = (a - high.astype(F32)).astype(BF16)
    return dot_nn(high, b) + dot_nn(low, b)


def body(
    ctx, wt, sp, stream, mod, head, nf, info, wo, wit,
    tgt_out, grad_out, loss_out,
    ctxp, w4, s4, srecv, strb, modb, headb, nfb, woutb, lifted, slope, hidden, dnsend, dnrecv,
    unitb, ubuf, gbuf, att, zbuf, tsend, trecv, gpb, tgb, g1, r1, g2, r2, g3, r3, g4s, g4r,
    lx, lt, lz, cz, send_sem, recv_sem,
):
    tp = lax.axis_index("tp")
    dp = lax.axis_index("dp")
    zh, c = lax.div(tp, 2), lax.rem(tp, 2)
    xy, zl = lax.div(dp, 4), lax.rem(dp, 4)
    x, y = lax.div(xy, 4), lax.rem(xy, 4)
    z = zh * 4 + zl
    sibling = zh * 2 + (1 - c)

    def plane(dx, dy):
        return lax.rem(x + dx, 4) * 4 + lax.rem(y + dy, 4)

    def other(v, d):
        return lax.rem(v + d, 4)

    barrier = pltpu.get_barrier_semaphore()
    partners = [(tp, plane(dx, dy) * 4 + zl) for dx, dy in XY]
    partners += [(lax.rem(tp + d, 8), dp) for d in range(1, 8)]
    for step in (1, 15):
        zz = lax.rem(z + step, 16)
        partners.append((lax.div(zz, 4) * 2 + c, xy * 4 + lax.rem(zz, 4)))
    partners += [(tp, xy * 4 + other(zl, d)) for d in (1, 2, 3)]
    for p_tp, p_dp in partners:
        pl.semaphore_signal(barrier, inc=1, device_id={"tp": p_tp, "dp": p_dp}, device_id_type=MESH)
    pl.semaphore_wait(barrier, len(partners))

    sends = []

    def send(src, dst, kind, index, to_tp, to_dp):
        copy = pltpu.make_async_remote_copy(
            src_ref=src, dst_ref=dst,
            send_sem=send_sem.at[len(sends)], recv_sem=recv_sem.at[BASE[kind] + index],
            device_id={"tp": to_tp, "dp": to_dp}, device_id_type=MESH,
        )
        copy.start()
        sends.append(copy)

    def arrived(dst, kind, index):
        pltpu.make_async_remote_copy(
            src_ref=dst, dst_ref=dst,
            send_sem=send_sem.at[0], recv_sem=recv_sem.at[BASE[kind] + index],
            device_id={"tp": tp, "dp": dp}, device_id_type=MESH,
        ).wait_recv()

    def to_plane(source, target, kind):
        for dx, dy in XY:
            p = plane(dx, dy)
            send(source(p), target.at[xy], kind, xy, tp, p * 4 + zl)

    def from_plane(target, kind):
        for dx, dy in XY:
            p = plane(dx, dy)
            arrived(target.at[p], kind, p)

    def gather_own(view, kind, base):
        for d in (1, 3, 2):
            px, py = other(x, d) * 4 + y, x * 4 + other(y, d)
            send(view(xy, None), view(xy, None), kind, base + xy * 2, tp, px * 4 + zl)
            send(view(xy, None), view(xy, None), kind, base + xy * 2, tp, py * 4 + zl)

    def gather_forward(view, kind, base):
        for d in (1, 3, 2):
            px, py = other(x, d) * 4 + y, x * 4 + other(y, d)
            arrived(view(px, None), kind, base + px * 2)
            for e in (1, 3, 2):
                send(view(px, 0), view(px, 0), kind, base + px * 2, tp, (x * 4 + other(y, e)) * 4 + zl)
            arrived(view(py, None), kind, base + py * 2)
            for e in (1, 3, 2):
                send(view(py, 1), view(py, 1), kind, base + py * 2 + 1, tp, (other(x, e) * 4 + y) * 4 + zl)

    def gather_last(view, kind, base):
        for dx in (1, 2, 3):
            for dy in (1, 2, 3):
                p = plane(dx, dy)
                arrived(view(p, 0), kind, base + p * 2)
                arrived(view(p, 1), kind, base + p * 2 + 1)

    def ctx_view(chunk):
        def view(source, half):
            if half is None:
                return ctxp.at[pl.ds(2 * chunk, 2), source]
            return ctxp.at[pl.ds(2 * chunk, 2), source, pl.ds(16 * half, 16)]

        return view

    def unit_view(source, half):
        if half is None:
            return unitb.at[source]
        return unitb.at[source, pl.ds(16 * half, 16)]

    def slot(kind, zz, core):
        if kind == 0:
            return w4.at[lax.div(zz, 4) * 2 + core, lax.rem(zz, 4)]
        return s4.at[core, lax.div(zz, 4), lax.rem(zz, 4)]

    def ring_send(kind, zz, hop, direction):
        to = lax.rem(z + (1 if direction == 0 else 15), 16)
        ref = slot(kind, zz, c)
        send(ref, ref, "ring", (kind * 2 + direction) * 9 + hop,
             lax.div(to, 4) * 2 + c, xy * 4 + lax.rem(to, 4))

    def sibling_send(kind, zz):
        ref = slot(kind, zz, c)
        send(ref, ref, "sib", kind * 16 + zz, sibling, dp)

    def ring_start(kind):
        ring_send(kind, z, 1, 0)
        ring_send(kind, z, 1, 1)
        sibling_send(kind, z)

    def ring_step(kind, hop):
        for direction, last in ((0, 8), (1, 7)):
            if hop > last:
                continue
            zz = lax.rem(z + (16 - hop if direction == 0 else hop), 16)
            arrived(slot(kind, zz, c), "ring", (kind * 2 + direction) * 9 + hop)
            if hop < last:
                ring_send(kind, zz, hop + 1, direction)
            sibling_send(kind, zz)

    def ring_last(kind):
        for zz in range(16):
            arrived(slot(kind, zz, 1 - c), "sib", kind * 16 + zz)

    ctxp[tp, xy] = ctx[tp]
    for d in (1, 2, 7, 6, 3, 5, 4):
        t = lax.rem(tp + d, 8)
        send(ctx.at[t], ctxp.at[tp, xy], "ctx", tp, t, dp)
    to_plane(lambda p: sp.at[p], srecv, "sp")
    srecv[xy] = sp[xy]
    w4[tp, zl] = wt[...]
    ring_start(0)
    nfb[xy] = nf[tp]
    to_plane(lambda p: nf.at[tp], nfb, "nf")
    woutb[zl, xy] = wo[...]
    headb[zl] = head[...]
    for d in (1, 2, 3):
        other_dp = xy * 4 + other(zl, d)
        send(wo, woutb.at[zl, xy], "wo1", zl, tp, other_dp)
        send(head, headb.at[zl], "head", zl, tp, other_dp)
    modb[xy] = mod[:, pl.ds(pl.multiple_of(xy * 256, 256), 256)]
    to_plane(lambda p: mod.at[:, pl.ds(pl.multiple_of(p * 256, 256), 256)], modb, "mod")
    rows = pl.ds(pl.multiple_of(tp * 32, 32), 32)
    own_stream = pltpu.make_async_copy(
        stream.at[rows, pl.ds(pl.multiple_of(xy * 256, 256), 256)], strb.at[xy], send_sem.at[N_SEND - 1]
    )
    own_stream.start()
    to_plane(lambda p: stream.at[rows, pl.ds(pl.multiple_of(p * 256, 256), 256)], strb, "st")

    def ctx_own(chunk_step):
        chunk = other(zh, chunk_step)
        if chunk_step == 0:
            arrived(ctxp.at[sibling, xy], "ctx", sibling)
        else:
            arrived(ctxp.at[2 * chunk, xy], "ctx", 2 * chunk)
            arrived(ctxp.at[2 * chunk + 1, xy], "ctx", 2 * chunk + 1)
        gather_own(ctx_view(chunk), "ag", chunk * 32)

    def ctx_forward(chunk_step):
        chunk = other(zh, chunk_step)
        gather_forward(ctx_view(chunk), "ag", chunk * 32)

    group = lax.div(lax.broadcasted_iota(jnp.int32, (16, 128), 1), 32)
    from_plane(srecv, "sp")
    for t in range(4):
        pieces = [srecv[4 * t + g].astype(F32) for g in range(4)]
        for q in range(4):
            tile = jnp.zeros((16, 128), F32)
            for g in range(4):
                shift = ((g - q) * 32) % 128
                moved = pltpu.roll(pieces[g], shift, 1) if shift else pieces[g]
                tile = jnp.where(group == g, moved, tile)
            hidden[8 * q : 8 * q + 8, 128 * t : 128 * t + 128] = tile[0:8]
            hidden[32 + 8 * q : 40 + 8 * q, 128 * t : 128 * t + 128] = tile[8:16]
    s4[c, zh, zl] = hidden[0:64, 0:512].astype(BF16)
    ring_start(1)

    ctx_own(0)

    def lift(block):
        piece = nfb[4 * block : 4 * block + 4].reshape(128, 256)
        for n in range(4):
            v = dot_nn(piece, wit[:, 512 * n : 512 * n + 512])
            v = v / (1.0 + jnp.exp(-v))
            lifted[128 * block : 128 * block + 128, 512 * n : 512 * n + 512] = v.astype(BF16)

    from_plane(nfb, "nf")
    ring_step(0, 1)
    ring_step(1, 1)
    lift(0)
    ctx_own(1)
    ctx_forward(0)
    ring_step(0, 2)
    ring_step(1, 2)
    lift(1)
    ctx_own(3)
    ctx_forward(1)
    for d in (1, 2, 3):
        zo = other(zl, d)
        arrived(woutb.at[zo, xy], "wo1", zo)
    for dx, dy in XY:
        p = plane(dx, dy)
        send(woutb.at[:, xy], woutb.at[:, xy], "wo2", xy, tp, p * 4 + zl)
    ring_step(0, 3)
    ring_step(1, 3)
    lift(2)
    ctx_own(2)
    ctx_forward(3)
    ring_step(0, 4)
    ring_step(1, 4)
    lift(3)
    ring_step(0, 5)
    ring_step(1, 5)
    ctx_forward(2)
    ring_step(0, 6)
    ring_step(1, 6)
    from_plane(modb, "mod")
    count_part = modb[0, 3:4, 0:128]
    for s in range(1, 16):
        count_part = count_part + modb[s, 3:4, 0:128]
    cz[zl] = jnp.broadcast_to(count_part, (8, 128))
    for d in (1, 2, 3):
        send(cz.at[zl], cz.at[zl], "cnt", zl, tp, xy * 4 + other(zl, d))
    for hop in (7, 8):
        ring_step(0, hop)
        ring_step(1, hop)
    ring_last(1)

    def up_part(zb):
        return s4[:, :, zb, 0:32, :].reshape(256, 512)

    def down_part(zb):
        return s4[:, :, zb, 32:64, :].reshape(256, 512)

    k0 = math.sqrt(2.0 / math.pi)
    for block in range(2):
        rs = slice(256 * block, 256 * block + 256)
        pre = dot_nt(lifted[rs, 0:512], up_part(0))
        for zb in range(1, 4):
            pre = pre + dot_nt(lifted[rs, 512 * zb : 512 * zb + 512], up_part(zb))
        tangent = jnp.tanh(k0 * (pre + 0.044715 * pre * pre * pre))
        slope[rs] = 0.5 * (1.0 + tangent) + 0.5 * pre * (1.0 - tangent * tangent) * k0 * (
            1.0 + 3.0 * 0.044715 * pre * pre
        )
        act = (0.5 * pre * (1.0 + tangent)).astype(BF16)
        for zb in range(4):
            part = dot_nn(act, down_part(zb)).astype(BF16)
            dnsend[8 * block : 8 * block + 8, :, 512 * zb : 512 * zb + 512] = part.reshape(8, 32, 512)
    dnrecv[xy] = dnsend[xy]
    to_plane(lambda p: dnsend.at[p], dnrecv, "dn")

    ring_last(0)
    for d in (1, 2, 3):
        zo = other(zl, d)
        arrived(headb.at[zo], "head", zo)
    from_plane(strb, "st")
    own_stream.wait()
    for step in (0, 1, 3, 2):
        gather_last(ctx_view(other(zh, step)), "ag", other(zh, step) * 32)
    att[...] = jnp.zeros_like(att)

    def att_step(t, carry):
        att[...] += dot_nt(ctxp[t].reshape(512, 512), w4[t].reshape(256, 512))
        return carry

    lax.fori_loop(0, 8, att_step, 0)
    lane = lax.broadcasted_iota(jnp.int32, (32, 128), 1)

    def norm_step(s, carry):
        state = strb[s].astype(F32) + modb[s, 0:1] * att[pl.ds(pl.multiple_of(s * 32, 32), 32)]
        center = jnp.mean(state, axis=-1, keepdims=True)
        state = state - center
        square = jnp.sum(state * state, axis=-1, keepdims=True)
        zbuf[s] = (state * (1.0 + modb[s, 2:3])).astype(BF16)
        tsend[s, 32:64] = jnp.where(lane < 64, center, square)
        return carry

    lax.fori_loop(0, 16, norm_step, 0)
    whole_head = headb[...].reshape(256, 128)
    tsend[:, 0:32] = dot_nn(zbuf[...].reshape(512, 256), whole_head).reshape(16, 32, 128)
    ones_row = (lax.broadcasted_iota(jnp.int32, (1, 8, 1), 1) == 2).astype(F32)
    vectors = (modb[...] + ones_row).reshape(128, 256)
    tsend[:, 64:72] = split_dot(vectors, whole_head).reshape(16, 8, 128)
    trecv[xy] = tsend[xy]
    to_plane(lambda p: tsend.at[p], trecv, "tm")

    from_plane(dnrecv, "dn")
    from_plane(_Columns(woutb), "wo2")
    own_nf = nf[tp]

    def down_sum(s, total):
        return total + dnrecv[s].astype(F32)

    mixed = dot_nn(own_nf, wit[...])
    mixed = lax.fori_loop(0, 16, down_sum, mixed)
    inv_rms = lax.rsqrt(jnp.mean(mixed * mixed, axis=-1, keepdims=True) + EPS)
    unit_b = (mixed * inv_rms).astype(BF16)
    unitb[xy] = unit_b
    gather_own(unit_view, "un", 0)
    whole_out = woutb[...].reshape(2048, 128)
    pred = dot_nn(unit_b, whole_out)
    gather_forward(unit_view, "un", 0)
    fold = dot_nn(down_part(0), whole_out[0:512])
    for zb in range(1, 4):
        fold = fold + dot_nn(down_part(zb), whole_out[512 * zb : 512 * zb + 512])
    gbuf[...] = fold.astype(BF16)

    for d in (1, 2, 3):
        zo = other(zl, d)
        arrived(cz.at[zo], "cnt", zo)
    count = cz[0, 0:1] + cz[1, 0:1] + cz[2, 0:1] + cz[3, 0:1]
    from_plane(trecv, "tm")
    velocity = trecv[0, 0:32]
    center = trecv[0, 32:64, 0:1]
    square = trecv[0, 32:64, 127:128]
    shift_row = trecv[0, 65:66]
    for s in range(1, 16):
        velocity = velocity + trecv[s, 0:32]
        center = center + trecv[s, 32:64, 0:1]
        square = square + trecv[s, 32:64, 127:128]
        shift_row = shift_row + trecv[s, 65:66]
    center = center * (1.0 / 16.0)
    for s in range(16):
        gap = trecv[s, 32:64, 0:1] - center
        square = square + 256.0 * gap * gap
        velocity = velocity + gap * trecv[s, 66:67]
    velocity = velocity * lax.rsqrt(square * (1.0 / 4096.0) + EPS) + shift_row
    target = info[0:1] * velocity + info[1:2] * own_nf[:, 0:128].astype(F32)
    tgb[tp] = target
    frame = (lax.broadcasted_iota(jnp.int32, (32, 128), 0) + tp * 32).astype(F32)
    live = (frame < info[2:3]).astype(F32)
    error = pred - target
    grad_pred = (LOSS_SCALE * 2.0 / (count * C)) * live * error
    along = jnp.sum(grad_pred * pred, axis=-1, keepdims=True) * (1.0 / 2048.0)
    gpb[xy, :, 0:128] = (inv_rms * grad_pred).astype(BF16)
    gpb[xy, :, 128:256] = jnp.broadcast_to(inv_rms * along, (32, 128)).astype(BF16)
    to_plane(lambda p: gpb.at[xy], gpb, "gp")
    lx[xy] = jnp.broadcast_to(jnp.sum(live * error * error), (8, 128))
    to_plane(lambda p: lx.at[xy], lx, "lx")
    for d in (1, 2, 7, 6, 3, 5, 4):
        send(tgb.at[tp], tgb.at[tp], "tg", tp, lax.rem(tp + d, 8), dp)

    gather_last(unit_view, "un", 0)
    for block in range(4):
        piece = unitb[4 * block : 4 * block + 4].reshape(128, 2048)
        along_down = dot_nt(piece[:, 0:512], down_part(0))
        for zb in range(1, 4):
            along_down = along_down + dot_nt(piece[:, 512 * zb : 512 * zb + 512], down_part(zb))
        ubuf[128 * block : 128 * block + 128] = along_down
    from_plane(gpb, "gp")
    both = gpb[...].reshape(512, 256)
    grad_hidden = dot_nt(both[:, 0:128], gbuf[...]) - both[:, 128:129].astype(F32) * ubuf[...]
    grad_pre = (grad_hidden * slope[...]).astype(BF16)
    for zb in range(4):
        g1[:, :, zb] = dot_tn(grad_pre, lifted[:, 512 * zb : 512 * zb + 512]).reshape(2, 4, 32, 512)
        send(g1.at[1 - c, :, zb], r1.at[:, zb], "g1", zb, sibling, dp)
    for zb in range(4):
        arrived(r1.at[:, zb], "g1", zb)
        g2[zb] = (g1[c, :, zb] + r1[:, zb]).astype(BF16)
    r2[zl] = g2[zl]
    for d in (1, 2, 3):
        zo = other(zl, d)
        send(g2.at[zo], r2.at[zl], "g2", zl, tp, xy * 4 + zo)
    from_plane(lx, "lx")
    loss_sum = lx[0]
    for s in range(1, 16):
        loss_sum = loss_sum + lx[s]
    lt[tp] = loss_sum
    for d in range(1, 8):
        send(lt.at[tp], lt.at[tp], "lt", tp, lax.rem(tp + d, 8), dp)
    for d in (1, 2, 3):
        zo = other(zl, d)
        arrived(r2.at[zo], "g2", zo)
    g3[...] = (r2[0].astype(F32) + r2[1].astype(F32) + r2[2].astype(F32) + r2[3].astype(F32)).astype(BF16)
    r3[zh] = g3[zh]
    for d in (1, 2, 3):
        ho = other(zh, d)
        send(g3.at[ho], r3.at[zh], "g3", zh, ho * 2 + c, dp)
    for d in range(1, 8):
        t = lax.rem(tp + d, 8)
        arrived(lt.at[t], "lt", t)
    loss_sum = lt[0]
    for s in range(1, 8):
        loss_sum = loss_sum + lt[s]
    lz[zl] = loss_sum
    for d in (1, 2, 3):
        send(lz.at[zl], lz.at[zl], "lz", zl, tp, xy * 4 + other(zl, d))
    for d in (1, 2, 3):
        ho = other(zh, d)
        arrived(r3.at[ho], "g3", ho)
    total = r3[0].astype(F32) + r3[1].astype(F32) + r3[2].astype(F32) + r3[3].astype(F32)
    group8 = lax.div(lax.broadcasted_iota(jnp.int32, (8, 128), 1), 32)
    for t in range(4):
        for g in range(4):
            tile = jnp.zeros((8, 128), F32)
            for q in range(4):
                shift = ((q - g) * 32) % 128
                piece = total[8 * q : 8 * q + 8, 128 * t : 128 * t + 128]
                moved = pltpu.roll(piece, shift, 1) if shift else piece
                tile = jnp.where(group8 == q, moved, tile)
            g4s[4 * t + g] = tile
    g4r[xy] = g4s[xy]
    to_plane(lambda p: g4s.at[p], g4r, "g4")
    for d in (1, 2, 3):
        zo = other(zl, d)
        arrived(lz.at[zo], "lz", zo)
    loss_out[...] = (lz[0] + lz[1] + lz[2] + lz[3]) / (count * C)
    for d in range(1, 8):
        t = lax.rem(tp + d, 8)
        arrived(tgb.at[t], "tg", t)
    tgt_out[...] = tgb[...]
    from_plane(g4r, "g4")
    grad_out[...] = g4r[...]
    for copy in sends:
        copy.wait_send()
    assert len(sends) < N_SEND


class _Columns:
    def __init__(self, ref):
        self.ref = ref

    @property
    def at(self):
        return self

    def __getitem__(self, p):
        return self.ref.at[:, p]


def call(*args):
    vmem = pl.BlockSpec(memory_space=pltpu.VMEM)
    hbm = pl.BlockSpec(memory_space=pl.ANY)
    V = pltpu.VMEM
    return pl.pallas_call(
        body,
        out_shape=(
            jax.ShapeDtypeStruct((8, 32, 128), F32),
            jax.ShapeDtypeStruct((16, 8, 128), F32),
            jax.ShapeDtypeStruct((8, 128), F32),
        ),
        in_specs=[vmem, vmem, vmem, hbm, vmem, vmem, vmem, vmem, vmem, vmem],
        out_specs=(vmem, vmem, vmem),
        scratch_shapes=[
            V((8, 16, 32, 512), BF16),
            V((8, 4, 64, 512), BF16),
            V((2, 4, 4, 64, 512), BF16),
            V((16, 16, 128), BF16),
            V((16, 32, 256), BF16),
            V((16, 8, 256), F32),
            V((4, 64, 128), BF16),
            V((16, 32, 256), BF16),
            V((4, 16, 32, 128), BF16),
            V((512, 2048), BF16),
            V((512, 256), F32),
            V((64, 512), F32),
            V((16, 32, 2048), BF16),
            V((16, 32, 2048), BF16),
            V((16, 32, 2048), BF16),
            V((512, 256), F32),
            V((256, 128), BF16),
            V((512, 256), F32),
            V((16, 32, 256), BF16),
            V((16, 72, 128), F32),
            V((16, 72, 128), F32),
            V((16, 32, 256), BF16),
            V((8, 32, 128), F32),
            V((2, 4, 4, 32, 512), F32),
            V((4, 4, 32, 512), F32),
            V((4, 4, 32, 512), BF16),
            V((4, 4, 32, 512), BF16),
            V((4, 32, 512), BF16),
            V((4, 32, 512), BF16),
            V((16, 8, 128), F32),
            V((16, 8, 128), F32),
            V((16, 8, 128), F32),
            V((8, 8, 128), F32),
            V((4, 8, 128), F32),
            V((4, 8, 128), F32),
            pltpu.SemaphoreType.DMA((N_SEND,)),
            pltpu.SemaphoreType.DMA((N_RECV,)),
        ],
        compiler_params=pltpu.CompilerParams(
            collective_id=0, has_side_effects=True, vmem_limit_bytes=56 * 1024 * 1024
        ),
    )(*args)


def time_features(timestep):
    half = FREQ // 2
    freq_index = jnp.arange(half, dtype=F32)
    rates = jnp.exp(-math.log(10000.0) * freq_index / half)
    angles = timestep.astype(F32)[:, None] * rates[None, :]
    return jnp.concatenate([jnp.sin(angles), jnp.cos(angles)], axis=1).astype(BF16)


def local(
    context, stream, w_attn_out, modulation, w_teacher_head, noisy, timestep, frames,
    w_in, w_time, w_up, w_down, w_out,
):
    phase = (timestep.astype(F32) / STEPS + 0.008) / 1.008 * (math.pi / 2)
    frames_f = frames.astype(F32)
    info = jnp.stack([jnp.cos(phase)[0], jnp.sin(phase)[0], frames_f[0]])
    info = jnp.broadcast_to(jnp.pad(info, (0, 5))[:, None], (8, 128))
    mod = jnp.concatenate(
        [modulation[0], jnp.broadcast_to(frames_f[:, None], (1, 4096)), jnp.zeros((4, 4096), F32)], axis=0
    )
    features = jnp.broadcast_to(time_features(timestep), (256, FREQ))
    nf = jnp.concatenate([noisy, features], axis=1).reshape(8, 32, 256)
    wit = jnp.concatenate([w_in, w_time], axis=0)
    wit = wit.reshape(256, 16, 4, 32).transpose(0, 2, 1, 3).reshape(256, 2048)
    up = w_up.reshape(32, 16, 4, 6).transpose(1, 3, 2, 0).reshape(16, 6, 128)
    down = w_down.reshape(16, 4, 6, 32).transpose(0, 2, 1, 3).reshape(16, 6, 128)
    gap = jnp.zeros((16, 2, 128), BF16)
    pieces = jnp.concatenate([up, gap, down, gap], axis=1)
    target, grad, loss = call(
        context.reshape(8, 32, 512), w_attn_out.T, pieces, stream, mod, w_teacher_head, nf, info, w_out, wit
    )
    grad = grad[:, 0:6].reshape(16, 6, 4, 32).transpose(3, 0, 2, 1).reshape(32, 384)
    return target.reshape(256, C), loss[0, 0], grad


def solution(mesh):
    in_specs = (
        P("dp", "tp"),
        P("dp", None),
        P("tp", "dp"),
        P("dp", None, None),
        P("dp", None),
        P("dp", None),
        P("dp"),
        P("dp"),
        P(),
        P(),
        P("dp", "tp"),
        P("tp", "dp"),
        P("dp", None),
    )
    out_specs = (P("dp", None), P(), P("dp", "tp"))
    return jax.shard_map(local, mesh=mesh, in_specs=in_specs, out_specs=out_specs, check_vma=False)
```

```python
import math

import jax
import jax.numpy as jnp
from jax import lax
from jax.experimental import pallas as pl
from jax.experimental.pallas import tpu as pltpu
from jax.sharding import PartitionSpec as P

C = 128
FREQ = 128
STEPS = 1000
LOSS_SCALE = 32768.0
EPS = 1e-06
F32 = jnp.float32
BF16 = jnp.bfloat16
MESH = pl.DeviceIdType.MESH
N_SEND = 520

COUNTS = dict(
    ctx=8, ag=128, ring=36, sib=32, sp=16, st=16, mod=16, head=4, nf=16, wo1=4, wo2=16, cnt=4,
    dnx=4, dny=4, dn2x=4, dn2y=4, fr=16, un=32, tm=16, gp=16, lx=16, tg=8, lt=8, lz=4, g1=4, g2=4, g3=4, g4=16,
)
BASE = {}
N_RECV = 0
for _name, _count in COUNTS.items():
    BASE[_name] = N_RECV
    N_RECV += _count

XY = [(dx, dy) for dx in range(4) for dy in range(4) if dx or dy]


def dot_nt(a, b):
    return lax.dot_general(a, b, (((1,), (1,)), ((), ())), preferred_element_type=F32)


def dot_nn(a, b):
    return jnp.dot(a, b, preferred_element_type=F32)


def dot_tn(a, b):
    return lax.dot_general(a, b, (((0,), (0,)), ((), ())), preferred_element_type=F32)


def split_dot(a, b):
    high = a.astype(BF16)
    low = (a - high.astype(F32)).astype(BF16)
    return dot_nn(high, b) + dot_nn(low, b)


def body(
    ctx, wa, wu, wd, stream, mod, head, noisy, info, wo, win, wtime,
    tgt_out, grad_out, loss_out,
    ctxp, w4, s4, sp, srecv, strb, modb, headb, nfb, woutb, wit, lifted, slope, hidden, dnsend,
    dnx, dny, sx, sy, dn2x, dn2y,
    unitb, ubuf, gbuf, att, zbuf, tsend, trecv, gpb, tgb, g1, r1, g2, r2, g3, r3, g4s, g4r,
    lx, lt, lz, fr, cz, send_sem, recv_sem,
):
    tp = lax.axis_index("tp")
    dp = lax.axis_index("dp")
    zh, c = lax.div(tp, 2), lax.rem(tp, 2)
    xy, zl = lax.div(dp, 4), lax.rem(dp, 4)
    x, y = lax.div(xy, 4), lax.rem(xy, 4)
    z = zh * 4 + zl
    sibling = zh * 2 + (1 - c)

    def plane(dx, dy):
        return lax.rem(x + dx, 4) * 4 + lax.rem(y + dy, 4)

    def other(v, d):
        return lax.rem(v + d, 4)

    barrier = pltpu.get_barrier_semaphore()
    partners = [(tp, plane(dx, dy) * 4 + zl) for dx, dy in XY]
    partners += [(lax.rem(tp + d, 8), dp) for d in range(1, 8)]
    for step in (1, 15):
        zz = lax.rem(z + step, 16)
        partners.append((lax.div(zz, 4) * 2 + c, xy * 4 + lax.rem(zz, 4)))
    partners += [(tp, xy * 4 + other(zl, d)) for d in (1, 2, 3)]
    for p_tp, p_dp in partners:
        pl.semaphore_signal(barrier, inc=1, device_id={"tp": p_tp, "dp": p_dp}, device_id_type=MESH)
    pl.semaphore_wait(barrier, len(partners))

    sends = []

    def send(src, dst, kind, index, to_tp, to_dp):
        copy = pltpu.make_async_remote_copy(
            src_ref=src, dst_ref=dst,
            send_sem=send_sem.at[len(sends)], recv_sem=recv_sem.at[BASE[kind] + index],
            device_id={"tp": to_tp, "dp": to_dp}, device_id_type=MESH,
        )
        copy.start()
        sends.append(copy)

    def arrived(dst, kind, index):
        pltpu.make_async_remote_copy(
            src_ref=dst, dst_ref=dst,
            send_sem=send_sem.at[0], recv_sem=recv_sem.at[BASE[kind] + index],
            device_id={"tp": tp, "dp": dp}, device_id_type=MESH,
        ).wait_recv()

    def to_plane(source, target, kind):
        for dx, dy in XY:
            p = plane(dx, dy)
            send(source(p), target.at[xy], kind, xy, tp, p * 4 + zl)

    def from_plane(target, kind):
        for dx, dy in XY:
            p = plane(dx, dy)
            arrived(target.at[p], kind, p)

    def gather_own(view, kind, base):
        for d in (1, 3, 2):
            px, py = other(x, d) * 4 + y, x * 4 + other(y, d)
            send(view(xy, None), view(xy, None), kind, base + xy * 2, tp, px * 4 + zl)
            send(view(xy, None), view(xy, None), kind, base + xy * 2, tp, py * 4 + zl)

    def gather_forward(view, kind, base):
        for d in (1, 3, 2):
            px, py = other(x, d) * 4 + y, x * 4 + other(y, d)
            arrived(view(px, None), kind, base + px * 2)
            for e in (1, 3, 2):
                send(view(px, 0), view(px, 0), kind, base + px * 2, tp, (x * 4 + other(y, e)) * 4 + zl)
            arrived(view(py, None), kind, base + py * 2)
            for e in (1, 3, 2):
                send(view(py, 1), view(py, 1), kind, base + py * 2 + 1, tp, (other(x, e) * 4 + y) * 4 + zl)

    def gather_last(view, kind, base):
        for dx in (1, 2, 3):
            for dy in (1, 2, 3):
                p = plane(dx, dy)
                arrived(view(p, 0), kind, base + p * 2)
                arrived(view(p, 1), kind, base + p * 2 + 1)

    def ctx_view(chunk):
        def view(source, half):
            if half is None:
                return ctxp.at[pl.ds(2 * chunk, 2), source]
            return ctxp.at[pl.ds(2 * chunk, 2), source, pl.ds(16 * half, 16)]

        return view

    def unit_view(source, half):
        if half is None:
            return unitb.at[source]
        return unitb.at[source, pl.ds(16 * half, 16)]

    def slot(kind, zz, core):
        if kind == 0:
            return w4.at[lax.div(zz, 4) * 2 + core, lax.rem(zz, 4)]
        return s4.at[core, lax.div(zz, 4), lax.rem(zz, 4)]

    def ring_send(kind, zz, hop, direction):
        to = lax.rem(z + (1 if direction == 0 else 15), 16)
        ref = slot(kind, zz, c)
        send(ref, ref, "ring", (kind * 2 + direction) * 9 + hop,
             lax.div(to, 4) * 2 + c, xy * 4 + lax.rem(to, 4))

    def sibling_send(kind, zz):
        ref = slot(kind, zz, c)
        send(ref, ref, "sib", kind * 16 + zz, sibling, dp)

    def ring_start(kind):
        ring_send(kind, z, 1, 0)
        ring_send(kind, z, 1, 1)
        sibling_send(kind, z)

    def ring_step(kind, hop):
        for direction, last in ((0, 8), (1, 7)):
            if hop > last:
                continue
            zz = lax.rem(z + (16 - hop if direction == 0 else hop), 16)
            arrived(slot(kind, zz, c), "ring", (kind * 2 + direction) * 9 + hop)
            if hop < last:
                ring_send(kind, zz, hop + 1, direction)
            sibling_send(kind, zz)

    def ring_last(kind):
        for zz in range(16):
            arrived(slot(kind, zz, 1 - c), "sib", kind * 16 + zz)

    ctxp[tp, xy] = ctx[tp]
    for d in (1, 2, 7, 6, 3, 5, 4):
        t = lax.rem(tp + d, 8)
        send(ctx.at[t], ctxp.at[tp, xy], "ctx", tp, t, dp)
    selects = [select_units(q) for q in range(4)]
    up = [dot_nt(selects[q], wu[...]) for q in range(4)]
    down = [dot_nn(selects[q], wd[...]) for q in range(4)]
    sp[:, 0:8] = jnp.concatenate(up, axis=1).reshape(16, 8, 128).astype(BF16)
    sp[:, 8:16] = jnp.concatenate(down, axis=1).reshape(16, 8, 128).astype(BF16)
    srecv[xy] = sp[xy]
    to_plane(lambda p: sp.at[p], srecv, "sp")
    nfb[xy, :, 0:128] = noisy[tp]
    nfb[xy, :, 128:256] = jnp.broadcast_to(info[3:4], (32, 128)).astype(BF16)
    to_plane(lambda p: nfb.at[xy], nfb, "nf")
    w4[tp, zl] = wa[...].astype(F32).T.astype(BF16)
    ring_start(0)
    woutb[zl, xy] = wo[...]
    headb[zl] = head[...]
    for d in (1, 2, 3):
        other_dp = xy * 4 + other(zl, d)
        send(wo, woutb.at[zl, xy], "wo1", zl, tp, other_dp)
        send(head, headb.at[zl], "head", zl, tp, other_dp)
    rows = pl.ds(pl.multiple_of(tp * 32, 32), 32)
    own_stream = pltpu.make_async_copy(
        stream.at[rows, pl.ds(pl.multiple_of(xy * 256, 256), 256)], strb.at[xy], send_sem.at[N_SEND - 1]
    )
    own_stream.start()

    def small_sends():
        modb[xy] = mod[0, :, pl.ds(pl.multiple_of(xy * 256, 256), 256)]
        to_plane(lambda p: mod.at[0, :, pl.ds(pl.multiple_of(p * 256, 256), 256)], modb, "mod")
        fr[xy] = jnp.broadcast_to(info[2:3], (8, 128))
        to_plane(lambda p: fr.at[xy], fr, "fr")
        to_plane(lambda p: stream.at[rows, pl.ds(pl.multiple_of(p * 256, 256), 256)], strb, "st")

    def ctx_own(chunk_step):
        chunk = other(zh, chunk_step)
        if chunk_step == 0:
            arrived(ctxp.at[sibling, xy], "ctx", sibling)
        else:
            arrived(ctxp.at[2 * chunk, xy], "ctx", 2 * chunk)
            arrived(ctxp.at[2 * chunk + 1, xy], "ctx", 2 * chunk + 1)
        gather_own(ctx_view(chunk), "ag", chunk * 32)

    def ctx_forward(chunk_step):
        chunk = other(zh, chunk_step)
        gather_forward(ctx_view(chunk), "ag", chunk * 32)

    group = lax.div(lax.broadcasted_iota(jnp.int32, (16, 128), 1), 32)
    from_plane(srecv, "sp")
    for t in range(4):
        pieces = [srecv[4 * t + g].astype(F32) for g in range(4)]
        for q in range(4):
            tile = jnp.zeros((16, 128), F32)
            for g in range(4):
                shift = ((g - q) * 32) % 128
                moved = pltpu.roll(pieces[g], shift, 1) if shift else pieces[g]
                tile = jnp.where(group == g, moved, tile)
            hidden[8 * q : 8 * q + 8, 128 * t : 128 * t + 128] = tile[0:8]
            hidden[32 + 8 * q : 40 + 8 * q, 128 * t : 128 * t + 128] = tile[8:16]
    s4[c, zh, zl] = hidden[0:64, 0:512].astype(BF16)
    ring_start(1)

    ctx_own(0)

    def lift(block):
        piece = nfb[4 * block : 4 * block + 4].reshape(128, 256)
        for n in range(4):
            v = dot_nn(piece, wit[:, 512 * n : 512 * n + 512])
            v = v / (1.0 + jnp.exp(-v))
            lifted[128 * block : 128 * block + 128, 512 * n : 512 * n + 512] = v.astype(BF16)

    def rings(hop):
        ring_step(1, hop)
        ring_step(0, hop)

    group128 = lax.div(lax.broadcasted_iota(jnp.int32, (128, 128), 1), 32)

    def order_features(zo):
        for half, source in ((0, win), (1, wtime)):
            for t in range(4):
                tile = jnp.zeros((128, 128), F32)
                for g in range(4):
                    piece = source[:, 128 * (4 * t + g) : 128 * (4 * t + g) + 128].astype(F32)
                    shift = ((g - zo) * 32) % 128
                    moved = pltpu.roll(piece, shift, 1) if shift else piece
                    tile = jnp.where(group128 == g, moved, tile)
                at = 512 * zo + 128 * t
                wit[128 * half : 128 * half + 128, at : at + 128] = tile.astype(BF16)

    order_features(0)
    order_features(1)
    rings(1)
    order_features(2)
    ctx_own(1)
    order_features(3)
    rings(2)
    from_plane(nfb, "nf")
    ctx_own(3)
    small_sends()
    lift(0)
    ctx_forward(0)
    rings(3)
    ctx_own(2)
    lift(1)
    ctx_forward(1)
    rings(4)
    for d in (1, 2, 3):
        zo = other(zl, d)
        arrived(woutb.at[zo, xy], "wo1", zo)
    for dx, dy in XY:
        p = plane(dx, dy)
        send(woutb.at[:, xy], woutb.at[:, xy], "wo2", xy, tp, p * 4 + zl)
    lift(2)
    rings(5)
    ctx_forward(3)
    lift(3)
    rings(6)
    from_plane(fr, "fr")
    count_part = fr[0]
    for s in range(1, 16):
        count_part = count_part + fr[s]
    cz[zl] = count_part
    for d in (1, 2, 3):
        send(cz.at[zl], cz.at[zl], "cnt", zl, tp, xy * 4 + other(zl, d))
    rings(7)
    ctx_forward(2)
    rings(8)
    ring_last(1)

    def up_part(zb):
        return s4[:, :, zb, 0:32, :].reshape(256, 512)

    def down_part(zb):
        return s4[:, :, zb, 32:64, :].reshape(256, 512)

    k0 = math.sqrt(2.0 / math.pi)
    for block in range(2):
        rs = slice(256 * block, 256 * block + 256)
        pre = dot_nt(lifted[rs, 0:512], up_part(0))
        for zb in range(1, 4):
            pre = pre + dot_nt(lifted[rs, 512 * zb : 512 * zb + 512], up_part(zb))
        tangent = jnp.tanh(k0 * (pre + 0.044715 * pre * pre * pre))
        slope[rs] = 0.5 * (1.0 + tangent) + 0.5 * pre * (1.0 - tangent * tangent) * k0 * (
            1.0 + 3.0 * 0.044715 * pre * pre
        )
        act = (0.5 * pre * (1.0 + tangent)).astype(BF16)
        for zb in range(4):
            part = dot_nn(act, down_part(zb)).astype(BF16)
            dnsend[2 * block : 2 * block + 2, :, :, 512 * zb : 512 * zb + 512] = part.reshape(2, 4, 32, 512)
    dnx[x] = dnsend[x, :, :, 0:1024]
    dny[y] = dnsend[:, y, :, 1024:2048]
    for d in (1, 3, 2):
        xo, yo = other(x, d), other(y, d)
        send(dnsend.at[xo, :, :, pl.ds(0, 1024)], dnx.at[x], "dnx", x, tp, (xo * 4 + y) * 4 + zl)
        send(dnsend.at[:, yo, :, pl.ds(1024, 1024)], dny.at[y], "dny", y, tp, (x * 4 + yo) * 4 + zl)

    ring_last(0)
    for d in (1, 2, 3):
        zo = other(zl, d)
        arrived(headb.at[zo], "head", zo)
    from_plane(strb, "st")
    from_plane(modb, "mod")
    own_stream.wait()
    for step in (0, 1, 3, 2):
        gather_last(ctx_view(other(zh, step)), "ag", other(zh, step) * 32)
    att[...] = jnp.zeros_like(att)

    def att_step(t, carry):
        att[...] += dot_nt(ctxp[t].reshape(512, 512), w4[t].reshape(256, 512))
        return carry

    lax.fori_loop(0, 8, att_step, 0)
    lane = lax.broadcasted_iota(jnp.int32, (32, 128), 1)

    def norm_step(s, carry):
        state = strb[s].astype(F32) + modb[s, 0:1] * att[pl.ds(pl.multiple_of(s * 32, 32), 32)]
        center = jnp.mean(state, axis=-1, keepdims=True)
        state = state - center
        square = jnp.sum(state * state, axis=-1, keepdims=True)
        zbuf[s] = (state * (1.0 + modb[s, 2:3])).astype(BF16)
        tsend[s, 32:64] = jnp.where(lane < 64, center, square)
        return carry

    lax.fori_loop(0, 16, norm_step, 0)
    whole_head = headb[...].reshape(256, 128)
    tsend[:, 0:32] = dot_nn(zbuf[...].reshape(512, 256), whole_head).reshape(16, 32, 128)
    vectors = jnp.concatenate([modb[:, 1], 1.0 + modb[:, 2]], axis=0)
    vectors = split_dot(vectors, whole_head)
    tsend[:, 65] = vectors[0:16]
    tsend[:, 66] = vectors[16:32]
    trecv[xy] = tsend[xy]
    to_plane(lambda p: tsend.at[p], trecv, "tm")

    for d in (1, 3, 2):
        xo, yo = other(x, d), other(y, d)
        arrived(dnx.at[xo], "dnx", xo)
        arrived(dny.at[yo], "dny", yo)
    for k in range(4):
        sx[k] = sum(dnx[o, k].astype(F32) for o in range(4)).astype(BF16)
        sy[k] = sum(dny[o, k].astype(F32) for o in range(4)).astype(BF16)
    dn2x[y] = sx[y]
    dn2y[x] = sy[x]
    for d in (1, 3, 2):
        xo, yo = other(x, d), other(y, d)
        send(sx.at[yo], dn2x.at[y], "dn2x", y, tp, (x * 4 + yo) * 4 + zl)
        send(sy.at[xo], dn2y.at[x], "dn2y", x, tp, (xo * 4 + y) * 4 + zl)
    from_plane(_Columns(woutb), "wo2")
    whole_out = woutb[...].reshape(2048, 128)
    fold = dot_nn(down_part(0), whole_out[0:512])
    for zb in range(1, 4):
        fold = fold + dot_nn(down_part(zb), whole_out[512 * zb : 512 * zb + 512])
    gbuf[...] = fold.astype(BF16)
    own_nf = nfb[xy]
    mixed = dot_nn(own_nf, wit[...])
    for d in (1, 3, 2):
        xo, yo = other(x, d), other(y, d)
        arrived(dn2x.at[yo], "dn2x", yo)
        arrived(dn2y.at[xo], "dn2y", xo)
    down_x = sum(dn2x[o].astype(F32) for o in range(4))
    down_y = sum(dn2y[o].astype(F32) for o in range(4))
    mixed = mixed + jnp.concatenate([down_x, down_y], axis=1)
    inv_rms = lax.rsqrt(jnp.mean(mixed * mixed, axis=-1, keepdims=True) + EPS)
    unit_b = (mixed * inv_rms).astype(BF16)
    unitb[xy] = unit_b
    gather_own(unit_view, "un", 0)
    pred = dot_nn(unit_b, whole_out)
    gather_forward(unit_view, "un", 0)

    for d in (1, 2, 3):
        zo = other(zl, d)
        arrived(cz.at[zo], "cnt", zo)
    count = cz[0, 0:1] + cz[1, 0:1] + cz[2, 0:1] + cz[3, 0:1]
    from_plane(trecv, "tm")
    velocity = trecv[0, 0:32]
    center = trecv[0, 32:64, 0:1]
    square = trecv[0, 32:64, 127:128]
    shift_row = trecv[0, 65:66]
    for s in range(1, 16):
        velocity = velocity + trecv[s, 0:32]
        center = center + trecv[s, 32:64, 0:1]
        square = square + trecv[s, 32:64, 127:128]
        shift_row = shift_row + trecv[s, 65:66]
    center = center * (1.0 / 16.0)
    for s in range(16):
        gap = trecv[s, 32:64, 0:1] - center
        square = square + 256.0 * gap * gap
        velocity = velocity + gap * trecv[s, 66:67]
    velocity = velocity * lax.rsqrt(square * (1.0 / 4096.0) + EPS) + shift_row
    target = info[0:1] * velocity + info[1:2] * own_nf[:, 0:128].astype(F32)
    tgb[tp] = target
    frame = (lax.broadcasted_iota(jnp.int32, (32, 128), 0) + tp * 32).astype(F32)
    live = (frame < info[2:3]).astype(F32)
    error = pred - target
    grad_pred = (LOSS_SCALE * 2.0 / (count * C)) * live * error
    along = jnp.sum(grad_pred * pred, axis=-1, keepdims=True) * (1.0 / 2048.0)
    gpb[xy, :, 0:128] = (inv_rms * grad_pred).astype(BF16)
    gpb[xy, :, 128:256] = jnp.broadcast_to(inv_rms * along, (32, 128)).astype(BF16)
    to_plane(lambda p: gpb.at[xy], gpb, "gp")
    lx[xy] = jnp.broadcast_to(jnp.sum(live * error * error), (8, 128))
    to_plane(lambda p: lx.at[xy], lx, "lx")
    for d in (1, 2, 7, 6, 3, 5, 4):
        send(tgb.at[tp], tgb.at[tp], "tg", tp, lax.rem(tp + d, 8), dp)

    gather_last(unit_view, "un", 0)
    for block in range(4):
        piece = unitb[4 * block : 4 * block + 4].reshape(128, 2048)
        along_down = dot_nt(piece[:, 0:512], down_part(0))
        for zb in range(1, 4):
            along_down = along_down + dot_nt(piece[:, 512 * zb : 512 * zb + 512], down_part(zb))
        ubuf[128 * block : 128 * block + 128] = along_down
    from_plane(gpb, "gp")
    both = gpb[...].reshape(512, 256)
    grad_hidden = dot_nt(both[:, 0:128], gbuf[...]) - both[:, 128:129].astype(F32) * ubuf[...]
    grad_pre = (grad_hidden * slope[...]).astype(BF16)
    for zb in range(4):
        g1[:, :, zb] = dot_tn(grad_pre, lifted[:, 512 * zb : 512 * zb + 512]).reshape(2, 4, 32, 512)
        send(g1.at[1 - c, :, zb], r1.at[:, zb], "g1", zb, sibling, dp)
    for zb in range(4):
        arrived(r1.at[:, zb], "g1", zb)
        g2[zb] = (g1[c, :, zb] + r1[:, zb]).astype(BF16)
    r2[zl] = g2[zl]
    for d in (1, 2, 3):
        zo = other(zl, d)
        send(g2.at[zo], r2.at[zl], "g2", zl, tp, xy * 4 + zo)
    from_plane(lx, "lx")
    loss_sum = lx[0]
    for s in range(1, 16):
        loss_sum = loss_sum + lx[s]
    lt[tp] = loss_sum
    for d in range(1, 8):
        send(lt.at[tp], lt.at[tp], "lt", tp, lax.rem(tp + d, 8), dp)
    for d in (1, 2, 3):
        zo = other(zl, d)
        arrived(r2.at[zo], "g2", zo)
    g3[...] = (r2[0].astype(F32) + r2[1].astype(F32) + r2[2].astype(F32) + r2[3].astype(F32)).astype(BF16)
    r3[zh] = g3[zh]
    for d in (1, 2, 3):
        ho = other(zh, d)
        send(g3.at[ho], r3.at[zh], "g3", zh, ho * 2 + c, dp)
    for d in range(1, 8):
        t = lax.rem(tp + d, 8)
        arrived(lt.at[t], "lt", t)
    loss_sum = lt[0]
    for s in range(1, 8):
        loss_sum = loss_sum + lt[s]
    lz[zl] = loss_sum
    for d in (1, 2, 3):
        send(lz.at[zl], lz.at[zl], "lz", zl, tp, xy * 4 + other(zl, d))
    for d in (1, 2, 3):
        ho = other(zh, d)
        arrived(r3.at[ho], "g3", ho)
    total = r3[0].astype(F32) + r3[1].astype(F32) + r3[2].astype(F32) + r3[3].astype(F32)
    group8 = lax.div(lax.broadcasted_iota(jnp.int32, (8, 128), 1), 32)
    for t in range(4):
        for g in range(4):
            tile = jnp.zeros((8, 128), F32)
            for q in range(4):
                shift = ((q - g) * 32) % 128
                piece = total[8 * q : 8 * q + 8, 128 * t : 128 * t + 128]
                moved = pltpu.roll(piece, shift, 1) if shift else piece
                tile = jnp.where(group8 == q, moved, tile)
            g4s[4 * t + g] = tile
    g4r[xy] = g4s[xy]
    to_plane(lambda p: g4s.at[p], g4r, "g4")
    for d in (1, 2, 3):
        zo = other(zl, d)
        arrived(lz.at[zo], "lz", zo)
    loss_out[...] = (lz[0] + lz[1] + lz[2] + lz[3]) / (count * C)
    for d in range(1, 8):
        t = lax.rem(tp + d, 8)
        arrived(tgb.at[t], "tg", t)
    tgt_out[...] = tgb[...]
    from_plane(g4r, "g4")
    part = g4r[...].reshape(128, 128)
    high = part.astype(BF16)
    part = part - high.astype(F32)
    middle = part.astype(BF16)
    low = (part - middle.astype(F32)).astype(BF16)
    grad = jnp.zeros((32, 384), F32)
    for q in range(4):
        chosen = dot_tn(high, selects[q]) + dot_tn(middle, selects[q]) + dot_tn(low, selects[q])
        grad = grad + chosen[32 * q : 32 * q + 32]
    grad_out[...] = grad
    for copy in sends:
        copy.wait_send()
    assert len(sends) < N_SEND


def select_units(q):
    row = lax.broadcasted_iota(jnp.int32, (128, 384), 0)
    unit = lax.broadcasted_iota(jnp.int32, (128, 384), 1)
    r = lax.rem(row, 8)
    chosen = (unit == lax.div(row, 8) * 24 + q * 6 + r) & (r < 6)
    return jnp.where(chosen, 1.0, 0.0).astype(BF16)


class _Columns:
    def __init__(self, ref):
        self.ref = ref

    @property
    def at(self):
        return self

    def __getitem__(self, p):
        return self.ref.at[:, p]


def call(*args):
    vmem = pl.BlockSpec(memory_space=pltpu.VMEM)
    hbm = pl.BlockSpec(memory_space=pl.ANY)
    V = pltpu.VMEM
    return pl.pallas_call(
        body,
        out_shape=(
            jax.ShapeDtypeStruct((8, 32, 128), F32),
            jax.ShapeDtypeStruct((32, 384), F32),
            jax.ShapeDtypeStruct((8, 128), F32),
        ),
        in_specs=[vmem] * 4 + [hbm] + [vmem] * 7,
        out_specs=(vmem, vmem, vmem),
        scratch_shapes=[
            V((8, 16, 32, 512), BF16),
            V((8, 4, 64, 512), BF16),
            V((2, 4, 4, 64, 512), BF16),
            V((16, 16, 128), BF16),
            V((16, 16, 128), BF16),
            V((16, 32, 256), BF16),
            V((16, 3, 256), F32),
            V((4, 64, 128), BF16),
            V((16, 32, 256), BF16),
            V((4, 16, 32, 128), BF16),
            V((256, 2048), BF16),
            V((512, 2048), BF16),
            V((512, 256), F32),
            V((64, 512), F32),
            V((4, 4, 32, 2048), BF16),
            V((4, 4, 32, 1024), BF16),
            V((4, 4, 32, 1024), BF16),
            V((4, 32, 1024), BF16),
            V((4, 32, 1024), BF16),
            V((4, 32, 1024), BF16),
            V((4, 32, 1024), BF16),
            V((16, 32, 2048), BF16),
            V((512, 256), F32),
            V((256, 128), BF16),
            V((512, 256), F32),
            V((16, 32, 256), BF16),
            V((16, 72, 128), F32),
            V((16, 72, 128), F32),
            V((16, 32, 256), BF16),
            V((8, 32, 128), F32),
            V((2, 4, 4, 32, 512), F32),
            V((4, 4, 32, 512), F32),
            V((4, 4, 32, 512), BF16),
            V((4, 4, 32, 512), BF16),
            V((4, 32, 512), BF16),
            V((4, 32, 512), BF16),
            V((16, 8, 128), F32),
            V((16, 8, 128), F32),
            V((16, 8, 128), F32),
            V((8, 8, 128), F32),
            V((4, 8, 128), F32),
            V((16, 8, 128), F32),
            V((4, 8, 128), F32),
            pltpu.SemaphoreType.DMA((N_SEND,)),
            pltpu.SemaphoreType.DMA((N_RECV,)),
        ],
        compiler_params=pltpu.CompilerParams(
            collective_id=0, has_side_effects=True, vmem_limit_bytes=56 * 1024 * 1024
        ),
    )(*args)


def time_features(timestep):
    half = FREQ // 2
    freq_index = jnp.arange(half, dtype=F32)
    rates = jnp.exp(-math.log(10000.0) * freq_index / half)
    angles = timestep.astype(F32)[:, None] * rates[None, :]
    return jnp.concatenate([jnp.sin(angles), jnp.cos(angles)], axis=1).astype(BF16)


def local(
    context, stream, w_attn_out, modulation, w_teacher_head, noisy, timestep, frames,
    w_in, w_time, w_up, w_down, w_out,
):
    phase = (timestep.astype(F32) / STEPS + 0.008) / 1.008 * (math.pi / 2)
    scalars = jnp.stack([jnp.cos(phase)[0], jnp.sin(phase)[0], frames.astype(F32)[0]])
    features = time_features(timestep).astype(F32)
    info = jnp.concatenate(
        [jnp.broadcast_to(scalars[:, None], (3, 128)), features, jnp.zeros((4, 128), F32)], axis=0
    )
    target, grad, loss = call(
        context.reshape(8, 32, 512), w_attn_out, w_up, w_down, stream, modulation, w_teacher_head,
        noisy.reshape(8, 32, 128), info, w_out, w_in, w_time,
    )
    return target.reshape(256, C), loss[0, 0], grad


def solution(mesh):
    in_specs = (
        P("dp", "tp"),
        P("dp", None),
        P("tp", "dp"),
        P("dp", None, None),
        P("dp", None),
        P("dp", None),
        P("dp"),
        P("dp"),
        P(),
        P(),
        P("dp", "tp"),
        P("tp", "dp"),
        P("dp", None),
    )
    out_specs = (P("dp", None), P(), P("dp", "tp"))
    return jax.shard_map(local, mesh=mesh, in_specs=in_specs, out_specs=out_specs, check_vma=False)
```

```python
import math

import jax
import jax.numpy as jnp
from jax import lax
from jax.experimental import pallas as pl
from jax.experimental.pallas import tpu as pltpu
from jax.sharding import PartitionSpec as P

C = 128
FREQ = 128
STEPS = 1000
LOSS_SCALE = 32768.0
EPS = 1e-06
F32 = jnp.float32
BF16 = jnp.bfloat16
MESH = pl.DeviceIdType.MESH
N_SEND = 520

COUNTS = dict(
    ctx=8, ag=128, ring=36, sib=32, sp=16, st=16, mod=16, head=4, nf=16, wo1=4, wo2=16, cnt=4,
    dnx=4, dny=4, dn2x=4, dn2y=4, un=32, tm=16, gp=16, lx=16, tg=8, lt=8, lz=4, g1=4, g2=4, g3=4, g4=16,
)
BASE = {}
N_RECV = 0
for _name, _count in COUNTS.items():
    BASE[_name] = N_RECV
    N_RECV += _count

XY = [(dx, dy) for dx in range(4) for dy in range(4) if dx or dy]


def dot_nt(a, b):
    return lax.dot_general(a, b, (((1,), (1,)), ((), ())), preferred_element_type=F32)


def dot_nn(a, b):
    return jnp.dot(a, b, preferred_element_type=F32)


def dot_tn(a, b):
    return lax.dot_general(a, b, (((0,), (0,)), ((), ())), preferred_element_type=F32)


def split_dot(a, b):
    high = a.astype(BF16)
    low = (a - high.astype(F32)).astype(BF16)
    return dot_nn(high, b) + dot_nn(low, b)


def body(
    ctx, wa, wu, wd, stream, mod, head, noisy, info, wo, win, wtime,
    tgt_out, grad_out, loss_out,
    ctxp, w4, s4, sp, srecv, strb, modb, headb, nfb, woutb, wit, lifted, slope, hidden, dnsend,
    dnx, dny, sx, sy, dn2x, dn2y,
    unitb, ubuf, gbuf, att, zbuf, tsend, trecv, gpb, tgb, g1, r1, g2, r2, g3, r3, g4s, g4r,
    lx, lt, lz, cz, send_sem, recv_sem,
):
    tp = lax.axis_index("tp")
    dp = lax.axis_index("dp")
    zh, c = lax.div(tp, 2), lax.rem(tp, 2)
    xy, zl = lax.div(dp, 4), lax.rem(dp, 4)
    x, y = lax.div(xy, 4), lax.rem(xy, 4)
    z = zh * 4 + zl
    sibling = zh * 2 + (1 - c)

    def plane(dx, dy):
        return lax.rem(x + dx, 4) * 4 + lax.rem(y + dy, 4)

    def other(v, d):
        return lax.rem(v + d, 4)

    barrier = pltpu.get_barrier_semaphore()
    partners = [(tp, plane(dx, dy) * 4 + zl) for dx, dy in XY]
    partners += [(lax.rem(tp + d, 8), dp) for d in range(1, 8)]
    for step in (1, 15):
        zz = lax.rem(z + step, 16)
        partners.append((lax.div(zz, 4) * 2 + c, xy * 4 + lax.rem(zz, 4)))
    partners += [(tp, xy * 4 + other(zl, d)) for d in (1, 2, 3)]
    for p_tp, p_dp in partners:
        pl.semaphore_signal(barrier, inc=1, device_id={"tp": p_tp, "dp": p_dp}, device_id_type=MESH)
    pl.semaphore_wait(barrier, len(partners))

    sends = []

    def send(src, dst, kind, index, to_tp, to_dp):
        copy = pltpu.make_async_remote_copy(
            src_ref=src, dst_ref=dst,
            send_sem=send_sem.at[len(sends)], recv_sem=recv_sem.at[BASE[kind] + index],
            device_id={"tp": to_tp, "dp": to_dp}, device_id_type=MESH,
        )
        copy.start()
        sends.append(copy)

    def arrived(dst, kind, index):
        pltpu.make_async_remote_copy(
            src_ref=dst, dst_ref=dst,
            send_sem=send_sem.at[0], recv_sem=recv_sem.at[BASE[kind] + index],
            device_id={"tp": tp, "dp": dp}, device_id_type=MESH,
        ).wait_recv()

    def to_plane(source, target, kind):
        for dx, dy in XY:
            p = plane(dx, dy)
            send(source(p), target.at[xy], kind, xy, tp, p * 4 + zl)

    def from_plane(target, kind):
        for dx, dy in XY:
            p = plane(dx, dy)
            arrived(target.at[p], kind, p)

    def gather_own(view, kind, base):
        for d in (1, 3, 2):
            px, py = other(x, d) * 4 + y, x * 4 + other(y, d)
            send(view(xy, None), view(xy, None), kind, base + xy * 2, tp, px * 4 + zl)
            send(view(xy, None), view(xy, None), kind, base + xy * 2, tp, py * 4 + zl)

    def gather_forward(view, kind, base):
        for d in (1, 3, 2):
            px, py = other(x, d) * 4 + y, x * 4 + other(y, d)
            arrived(view(px, None), kind, base + px * 2)
            for e in (1, 3, 2):
                send(view(px, 0), view(px, 0), kind, base + px * 2, tp, (x * 4 + other(y, e)) * 4 + zl)
            arrived(view(py, None), kind, base + py * 2)
            for e in (1, 3, 2):
                send(view(py, 1), view(py, 1), kind, base + py * 2 + 1, tp, (other(x, e) * 4 + y) * 4 + zl)

    def gather_last(view, kind, base):
        for dx in (1, 2, 3):
            for dy in (1, 2, 3):
                p = plane(dx, dy)
                arrived(view(p, 0), kind, base + p * 2)
                arrived(view(p, 1), kind, base + p * 2 + 1)

    def ctx_view(chunk):
        def view(source, half):
            if half is None:
                return ctxp.at[pl.ds(2 * chunk, 2), source]
            return ctxp.at[pl.ds(2 * chunk, 2), source, pl.ds(16 * half, 16)]

        return view

    def unit_view(source, half):
        if half is None:
            return unitb.at[source]
        return unitb.at[source, pl.ds(16 * half, 16)]

    def slot(kind, zz, core):
        if kind == 0:
            return w4.at[lax.div(zz, 4) * 2 + core, lax.rem(zz, 4)]
        return s4.at[core, lax.div(zz, 4), lax.rem(zz, 4)]

    def ring_send(kind, zz, hop, direction):
        to = lax.rem(z + (1 if direction == 0 else 15), 16)
        ref = slot(kind, zz, c)
        send(ref, ref, "ring", (kind * 2 + direction) * 9 + hop,
             lax.div(to, 4) * 2 + c, xy * 4 + lax.rem(to, 4))

    def sibling_send(kind, zz):
        ref = slot(kind, zz, c)
        send(ref, ref, "sib", kind * 16 + zz, sibling, dp)

    def ring_start(kind):
        ring_send(kind, z, 1, 0)
        ring_send(kind, z, 1, 1)
        sibling_send(kind, z)

    def ring_step(kind, hop):
        for direction, last in ((0, 8), (1, 7)):
            if hop > last:
                continue
            zz = lax.rem(z + (16 - hop if direction == 0 else hop), 16)
            arrived(slot(kind, zz, c), "ring", (kind * 2 + direction) * 9 + hop)
            if hop < last:
                ring_send(kind, zz, hop + 1, direction)
            sibling_send(kind, zz)

    def ring_last(kind):
        for zz in range(16):
            arrived(slot(kind, zz, 1 - c), "sib", kind * 16 + zz)

    ctxp[tp, xy] = ctx[tp]
    for d in (1, 2, 7, 6, 3, 5, 4):
        t = lax.rem(tp + d, 8)
        send(ctx.at[t], ctxp.at[tp, xy], "ctx", tp, t, dp)
    selects = [select_units(q) for q in range(4)]
    up = [dot_nt(selects[q], wu[...]) for q in range(4)]
    down = [dot_nt(selects[q], wd[...]) for q in range(4)]
    sp[:, 0:8] = jnp.concatenate(up, axis=1).reshape(16, 8, 128).astype(BF16)
    sp[:, 8:16] = jnp.concatenate(down, axis=1).reshape(16, 8, 128).astype(BF16)
    srecv[xy] = sp[xy]
    to_plane(lambda p: sp.at[p], srecv, "sp")
    nfb[xy, 0:32, 0:128] = noisy[tp]
    nfb[xy, 0:32, 128:256] = jnp.broadcast_to(info[3:4], (32, 128)).astype(BF16)
    nfb[xy, 32:48, 0:128] = jnp.broadcast_to(info[2:3], (16, 128)).astype(BF16)
    nfb[xy, 32:48, 128:256] = jnp.zeros((16, 128), BF16)
    to_plane(lambda p: nfb.at[xy], nfb, "nf")
    w4[tp, zl] = wa[...]
    ring_start(0)
    woutb[zl, xy] = wo[...]
    headb[zl] = head[...]
    for d in (1, 2, 3):
        other_dp = xy * 4 + other(zl, d)
        send(wo, woutb.at[zl, xy], "wo1", zl, tp, other_dp)
        send(head, headb.at[zl], "head", zl, tp, other_dp)
    rows = pl.ds(pl.multiple_of(tp * 32, 32), 32)
    own_stream = pltpu.make_async_copy(
        stream.at[rows, pl.ds(pl.multiple_of(xy * 256, 256), 256)], strb.at[xy], send_sem.at[N_SEND - 1]
    )
    own_stream.start()

    def small_sends():
        modb[xy] = mod[:, :, pl.ds(pl.multiple_of(xy * 256, 256), 256)]
        to_plane(lambda p: mod.at[:, :, pl.ds(pl.multiple_of(p * 256, 256), 256)], modb, "mod")
        to_plane(lambda p: stream.at[rows, pl.ds(pl.multiple_of(p * 256, 256), 256)], strb, "st")

    def ctx_own(chunk_step):
        chunk = other(zh, chunk_step)
        if chunk_step == 0:
            arrived(ctxp.at[sibling, xy], "ctx", sibling)
        else:
            arrived(ctxp.at[2 * chunk, xy], "ctx", 2 * chunk)
            arrived(ctxp.at[2 * chunk + 1, xy], "ctx", 2 * chunk + 1)
        gather_own(ctx_view(chunk), "ag", chunk * 32)

    def ctx_forward(chunk_step):
        chunk = other(zh, chunk_step)
        gather_forward(ctx_view(chunk), "ag", chunk * 32)

    group = lax.div(lax.broadcasted_iota(jnp.int32, (16, 128), 1), 32)
    from_plane(srecv, "sp")
    for t in range(4):
        pieces = [srecv[4 * t + g].astype(F32) for g in range(4)]
        for q in range(4):
            tile = jnp.zeros((16, 128), F32)
            for g in range(4):
                shift = ((g - q) * 32) % 128
                moved = pltpu.roll(pieces[g], shift, 1) if shift else pieces[g]
                tile = jnp.where(group == g, moved, tile)
            hidden[8 * q : 8 * q + 8, 128 * t : 128 * t + 128] = tile[0:8]
            hidden[32 + 8 * q : 40 + 8 * q, 128 * t : 128 * t + 128] = tile[8:16]
    s4[c, zh, zl] = hidden[0:64, 0:512].astype(BF16)
    ring_start(1)

    ctx_own(0)

    def lift(block):
        piece = nfb[4 * block : 4 * block + 4, 0:32].reshape(128, 256)
        for n in range(4):
            v = dot_nn(piece, wit[:, 512 * n : 512 * n + 512])
            v = v / (1.0 + jnp.exp(-v))
            lifted[128 * block : 128 * block + 128, 512 * n : 512 * n + 512] = v.astype(BF16)

    group128 = lax.div(lax.broadcasted_iota(jnp.int32, (128, 128), 1), 32)

    def order_features(zo):
        for half, source in ((0, win), (1, wtime)):
            for t in range(4):
                tile = jnp.zeros((128, 128), F32)
                for g in range(4):
                    piece = source[:, 128 * (4 * t + g) : 128 * (4 * t + g) + 128].astype(F32)
                    shift = ((g - zo) * 32) % 128
                    moved = pltpu.roll(piece, shift, 1) if shift else piece
                    tile = jnp.where(group128 == g, moved, tile)
                at = 512 * zo + 128 * t
                wit[128 * half : 128 * half + 128, at : at + 128] = tile.astype(BF16)

    k0 = math.sqrt(2.0 / math.pi)

    def up_part(zb):
        return s4[:, :, zb, 0:32, :].reshape(256, 512)

    def down_part(zb):
        return s4[:, :, zb, 32:64, :].reshape(256, 512)

    def student(block):
        rs = slice(256 * block, 256 * block + 256)
        pre = dot_nt(lifted[rs, 0:512], up_part(0))
        for zb in range(1, 4):
            pre = pre + dot_nt(lifted[rs, 512 * zb : 512 * zb + 512], up_part(zb))
        tangent = jnp.tanh(k0 * (pre + 0.044715 * pre * pre * pre))
        slope[rs] = 0.5 * (1.0 + tangent) + 0.5 * pre * (1.0 - tangent * tangent) * k0 * (
            1.0 + 3.0 * 0.044715 * pre * pre
        )
        act = (0.5 * pre * (1.0 + tangent)).astype(BF16)
        for zb in range(4):
            part = dot_nn(act, down_part(zb)).astype(BF16)
            dnsend[2 * block : 2 * block + 2, :, :, 512 * zb : 512 * zb + 512] = part.reshape(2, 4, 32, 512)

    def share_out():
        for d in (1, 2, 3):
            zo = other(zl, d)
            arrived(woutb.at[zo, xy], "wo1", zo)
        for dx, dy in XY:
            p = plane(dx, dy)
            send(woutb.at[:, xy], woutb.at[:, xy], "wo2", xy, tp, p * 4 + zl)

    def share_count():
        count_part = nfb[0, 32:40, 0:128].astype(F32)
        for s in range(1, 16):
            count_part = count_part + nfb[s, 32:40, 0:128].astype(F32)
        cz[zl] = count_part
        for d in (1, 2, 3):
            send(cz.at[zl], cz.at[zl], "cnt", zl, tp, xy * 4 + other(zl, d))

    small_sends()
    order_features(0)
    ring_step(1, 1)
    ring_step(0, 1)
    ctx_own(1)
    order_features(1)
    ring_step(1, 2)
    ring_step(0, 2)
    ctx_own(3)
    order_features(2)
    order_features(3)
    ring_step(1, 3)
    ring_step(0, 3)
    share_out()
    ctx_own(2)
    from_plane(nfb, "nf")
    ctx_forward(0)
    ring_step(1, 4)
    ring_step(0, 4)
    lift(0)
    lift(1)
    ctx_forward(1)
    ring_step(1, 5)
    ring_step(0, 5)
    lift(2)
    lift(3)
    ring_step(1, 6)
    ring_step(0, 6)
    ctx_forward(3)
    share_count()
    ring_step(1, 7)
    ring_step(0, 7)
    ctx_forward(2)
    ring_step(1, 8)
    ring_step(0, 8)
    ring_last(1)
    student(0)
    student(1)
    for d in (1, 3, 2):
        xo, yo = other(x, d), other(y, d)
        send(dnsend.at[xo, :, :, pl.ds(0, 1024)], dnx.at[x], "dnx", x, tp, (xo * 4 + y) * 4 + zl)
        send(dnsend.at[:, yo, :, pl.ds(1024, 1024)], dny.at[y], "dny", y, tp, (x * 4 + yo) * 4 + zl)
    dnx[x] = dnsend[x, :, :, 0:1024]
    dny[y] = dnsend[:, y, :, 1024:2048]
    ring_last(0)
    for d in (1, 3, 2):
        xo, yo = other(x, d), other(y, d)
        arrived(dnx.at[xo], "dnx", xo)
        arrived(dny.at[yo], "dny", yo)
    for k in range(4):
        sx[k] = sum(dnx[o, k].astype(F32) for o in range(4)).astype(BF16)
        sy[k] = sum(dny[o, k].astype(F32) for o in range(4)).astype(BF16)
    dn2x[y] = sx[y]
    dn2y[x] = sy[x]
    for d in (1, 3, 2):
        xo, yo = other(x, d), other(y, d)
        send(sx.at[yo], dn2x.at[y], "dn2x", y, tp, (x * 4 + yo) * 4 + zl)
        send(sy.at[xo], dn2y.at[x], "dn2y", x, tp, (xo * 4 + y) * 4 + zl)

    for d in (1, 2, 3):
        zo = other(zl, d)
        arrived(headb.at[zo], "head", zo)
    for step in (0, 1, 3, 2):
        gather_last(ctx_view(other(zh, step)), "ag", other(zh, step) * 32)
    att[...] = jnp.zeros_like(att)

    def att_step(t, carry):
        att[...] += dot_nt(ctxp[t].reshape(512, 512), w4[t].reshape(256, 512))
        return carry

    lax.fori_loop(0, 8, att_step, 0)

    from_plane(_Columns(woutb), "wo2")
    whole_out = woutb[...].reshape(2048, 128)
    fold = dot_nn(down_part(0), whole_out[0:512])
    for zb in range(1, 4):
        fold = fold + dot_nn(down_part(zb), whole_out[512 * zb : 512 * zb + 512])
    gbuf[...] = fold.astype(BF16)
    own_nf = nfb[xy, 0:32]
    mixed = dot_nn(own_nf, wit[...])
    for d in (1, 3, 2):
        xo, yo = other(x, d), other(y, d)
        arrived(dn2x.at[yo], "dn2x", yo)
        arrived(dn2y.at[xo], "dn2y", xo)
    down_x = sum(dn2x[o].astype(F32) for o in range(4))
    down_y = sum(dn2y[o].astype(F32) for o in range(4))
    mixed = mixed + jnp.concatenate([down_x, down_y], axis=1)
    inv_rms = lax.rsqrt(jnp.mean(mixed * mixed, axis=-1, keepdims=True) + EPS)
    unit_b = (mixed * inv_rms).astype(BF16)
    unitb[xy] = unit_b
    gather_own(unit_view, "un", 0)
    pred = dot_nn(unit_b, whole_out)

    from_plane(strb, "st")
    from_plane(modb, "mod")
    own_stream.wait()
    lane = lax.broadcasted_iota(jnp.int32, (32, 128), 1)

    def norm_step(s, carry):
        state = strb[s].astype(F32) + modb[s, 0] * att[pl.ds(pl.multiple_of(s * 32, 32), 32)]
        center = jnp.mean(state, axis=-1, keepdims=True)
        state = state - center
        square = jnp.sum(state * state, axis=-1, keepdims=True)
        zbuf[s] = (state * (1.0 + modb[s, 2])).astype(BF16)
        tsend[s, 32:64] = jnp.where(lane < 64, center, square)
        return carry

    lax.fori_loop(0, 16, norm_step, 0)
    whole_head = headb[...].reshape(256, 128)
    tsend[:, 0:32] = dot_nn(zbuf[...].reshape(512, 256), whole_head).reshape(16, 32, 128)
    vectors = jnp.concatenate([modb[:, 1, 0], 1.0 + modb[:, 2, 0]], axis=0)
    vectors = split_dot(vectors, whole_head)
    tsend[:, 65] = vectors[0:16]
    tsend[:, 66] = vectors[16:32]
    trecv[xy] = tsend[xy]
    to_plane(lambda p: tsend.at[p], trecv, "tm")
    gather_forward(unit_view, "un", 0)


    for d in (1, 2, 3):
        zo = other(zl, d)
        arrived(cz.at[zo], "cnt", zo)
    count = cz[0, 0:1] + cz[1, 0:1] + cz[2, 0:1] + cz[3, 0:1]
    from_plane(trecv, "tm")
    velocity = trecv[0, 0:32]
    center = trecv[0, 32:64, 0:1]
    square = trecv[0, 32:64, 127:128]
    shift_row = trecv[0, 65:66]
    for s in range(1, 16):
        velocity = velocity + trecv[s, 0:32]
        center = center + trecv[s, 32:64, 0:1]
        square = square + trecv[s, 32:64, 127:128]
        shift_row = shift_row + trecv[s, 65:66]
    center = center * (1.0 / 16.0)
    for s in range(16):
        gap = trecv[s, 32:64, 0:1] - center
        square = square + 256.0 * gap * gap
        velocity = velocity + gap * trecv[s, 66:67]
    velocity = velocity * lax.rsqrt(square * (1.0 / 4096.0) + EPS) + shift_row
    target = info[0:1] * velocity + info[1:2] * own_nf[:, 0:128].astype(F32)
    tgb[tp] = target
    frame = (lax.broadcasted_iota(jnp.int32, (32, 128), 0) + tp * 32).astype(F32)
    live = (frame < info[2:3]).astype(F32)
    error = pred - target
    grad_pred = (LOSS_SCALE * 2.0 / (count * C)) * live * error
    along = jnp.sum(grad_pred * pred, axis=-1, keepdims=True) * (1.0 / 2048.0)
    gpb[xy, :, 0:128] = (inv_rms * grad_pred).astype(BF16)
    gpb[xy, :, 128:256] = jnp.broadcast_to(inv_rms * along, (32, 128)).astype(BF16)
    to_plane(lambda p: gpb.at[xy], gpb, "gp")
    lx[xy] = jnp.broadcast_to(jnp.sum(live * error * error), (8, 128))
    to_plane(lambda p: lx.at[xy], lx, "lx")
    for d in (1, 2, 7, 6, 3, 5, 4):
        send(tgb.at[tp], tgb.at[tp], "tg", tp, lax.rem(tp + d, 8), dp)

    gather_last(unit_view, "un", 0)
    for block in range(4):
        piece = unitb[4 * block : 4 * block + 4].reshape(128, 2048)
        along_down = dot_nt(piece[:, 0:512], down_part(0))
        for zb in range(1, 4):
            along_down = along_down + dot_nt(piece[:, 512 * zb : 512 * zb + 512], down_part(zb))
        ubuf[128 * block : 128 * block + 128] = along_down
    from_plane(gpb, "gp")
    both = gpb[...].reshape(512, 256)
    grad_hidden = dot_nt(both[:, 0:128], gbuf[...]) - both[:, 128:129].astype(F32) * ubuf[...]
    grad_pre = (grad_hidden * slope[...]).astype(BF16)

    def both_cores(zb):
        arrived(r1.at[zb], "g1", zb)
        g2[zb] = (g1[zb, c] + r1[zb]).astype(BF16)
        if zb is not zl:
            send(g2.at[zb], r2.at[zl], "g2", zl, tp, xy * 4 + zb)

    previous = None
    for d in (2, 1, 3, 0):
        zb = other(zl, d) if d else zl
        columns = pl.ds(pl.multiple_of(zb * 512, 512), 512)
        g1[zb] = dot_tn(grad_pre, lifted[:, columns]).reshape(2, 4, 32, 512)
        send(g1.at[zb, 1 - c], r1.at[zb], "g1", zb, sibling, dp)
        if previous is not None:
            both_cores(previous)
        previous = zb
    both_cores(zl)
    r2[zl] = g2[zl]
    from_plane(lx, "lx")
    loss_sum = lx[0]
    for s in range(1, 16):
        loss_sum = loss_sum + lx[s]
    lt[tp] = loss_sum
    for d in range(1, 8):
        send(lt.at[tp], lt.at[tp], "lt", tp, lax.rem(tp + d, 8), dp)
    for d in (1, 2, 3):
        zo = other(zl, d)
        arrived(r2.at[zo], "g2", zo)
    g3[...] = (r2[0].astype(F32) + r2[1].astype(F32) + r2[2].astype(F32) + r2[3].astype(F32)).astype(BF16)
    r3[zh] = g3[zh]
    for d in (1, 2, 3):
        ho = other(zh, d)
        send(g3.at[ho], r3.at[zh], "g3", zh, ho * 2 + c, dp)
    for d in range(1, 8):
        t = lax.rem(tp + d, 8)
        arrived(lt.at[t], "lt", t)
    loss_sum = lt[0]
    for s in range(1, 8):
        loss_sum = loss_sum + lt[s]
    lz[zl] = loss_sum
    for d in (1, 2, 3):
        send(lz.at[zl], lz.at[zl], "lz", zl, tp, xy * 4 + other(zl, d))
    for d in (1, 2, 3):
        ho = other(zh, d)
        arrived(r3.at[ho], "g3", ho)
    total = r3[0].astype(F32) + r3[1].astype(F32) + r3[2].astype(F32) + r3[3].astype(F32)
    group8 = lax.div(lax.broadcasted_iota(jnp.int32, (8, 128), 1), 32)
    for t in range(4):
        for g in range(4):
            tile = jnp.zeros((8, 128), F32)
            for q in range(4):
                shift = ((q - g) * 32) % 128
                piece = total[8 * q : 8 * q + 8, 128 * t : 128 * t + 128]
                moved = pltpu.roll(piece, shift, 1) if shift else piece
                tile = jnp.where(group8 == q, moved, tile)
            g4s[4 * t + g] = tile
    g4r[xy] = g4s[xy]
    to_plane(lambda p: g4s.at[p], g4r, "g4")
    for d in (1, 2, 3):
        zo = other(zl, d)
        arrived(lz.at[zo], "lz", zo)
    loss_out[...] = (lz[0] + lz[1] + lz[2] + lz[3]) / (count * C)
    for d in range(1, 8):
        t = lax.rem(tp + d, 8)
        arrived(tgb.at[t], "tg", t)
    tgt_out[...] = tgb[...]
    from_plane(g4r, "g4")
    part = g4r[...].reshape(128, 128)
    high = part.astype(BF16)
    part = part - high.astype(F32)
    middle = part.astype(BF16)
    low = (part - middle.astype(F32)).astype(BF16)
    grad = jnp.zeros((32, 384), F32)
    for q in range(4):
        chosen = dot_tn(high, selects[q]) + dot_tn(middle, selects[q]) + dot_tn(low, selects[q])
        grad = grad + chosen[32 * q : 32 * q + 32]
    grad_out[...] = grad
    for copy in sends:
        copy.wait_send()
    assert len(sends) < N_SEND


def select_units(q):
    row = lax.broadcasted_iota(jnp.int32, (128, 384), 0)
    unit = lax.broadcasted_iota(jnp.int32, (128, 384), 1)
    r = lax.rem(row, 8)
    chosen = (unit == lax.div(row, 8) * 24 + q * 6 + r) & (r < 6)
    return jnp.where(chosen, 1.0, 0.0).astype(BF16)


class _Columns:
    def __init__(self, ref):
        self.ref = ref

    @property
    def at(self):
        return self

    def __getitem__(self, p):
        return self.ref.at[:, p]


def call(*args):
    vmem = pl.BlockSpec(memory_space=pltpu.VMEM)
    hbm = pl.BlockSpec(memory_space=pl.ANY)
    V = pltpu.VMEM
    return pl.pallas_call(
        body,
        out_shape=(
            jax.ShapeDtypeStruct((8, 32, 128), F32),
            jax.ShapeDtypeStruct((32, 384), F32),
            jax.ShapeDtypeStruct((8, 128), F32),
        ),
        in_specs=[vmem] * 4 + [hbm] + [vmem] * 7,
        out_specs=(vmem, vmem, vmem),
        scratch_shapes=[
            V((8, 16, 32, 512), BF16),
            V((8, 4, 64, 512), BF16),
            V((2, 4, 4, 64, 512), BF16),
            V((16, 16, 128), BF16),
            V((16, 16, 128), BF16),
            V((16, 32, 256), BF16),
            V((16, 3, 1, 256), F32),
            V((4, 64, 128), BF16),
            V((16, 48, 256), BF16),
            V((4, 16, 32, 128), BF16),
            V((256, 2048), BF16),
            V((512, 2048), BF16),
            V((512, 256), F32),
            V((64, 512), F32),
            V((4, 4, 32, 2048), BF16),
            V((4, 4, 32, 1024), BF16),
            V((4, 4, 32, 1024), BF16),
            V((4, 32, 1024), BF16),
            V((4, 32, 1024), BF16),
            V((4, 32, 1024), BF16),
            V((4, 32, 1024), BF16),
            V((16, 32, 2048), BF16),
            V((512, 256), F32),
            V((256, 128), BF16),
            V((512, 256), F32),
            V((16, 32, 256), BF16),
            V((16, 72, 128), F32),
            V((16, 72, 128), F32),
            V((16, 32, 256), BF16),
            V((8, 32, 128), F32),
            V((4, 2, 4, 32, 512), F32),
            V((4, 4, 32, 512), F32),
            V((4, 4, 32, 512), BF16),
            V((4, 4, 32, 512), BF16),
            V((4, 32, 512), BF16),
            V((4, 32, 512), BF16),
            V((16, 8, 128), F32),
            V((16, 8, 128), F32),
            V((16, 8, 128), F32),
            V((8, 8, 128), F32),
            V((4, 8, 128), F32),
            V((4, 8, 128), F32),
            pltpu.SemaphoreType.DMA((N_SEND,)),
            pltpu.SemaphoreType.DMA((N_RECV,)),
        ],
        compiler_params=pltpu.CompilerParams(
            collective_id=0, has_side_effects=True, vmem_limit_bytes=56 * 1024 * 1024
        ),
    )(*args)


def time_features(timestep):
    half = FREQ // 2
    freq_index = jnp.arange(half, dtype=F32)
    rates = jnp.exp(-math.log(10000.0) * freq_index / half)
    angles = timestep.astype(F32)[:, None] * rates[None, :]
    return jnp.concatenate([jnp.sin(angles), jnp.cos(angles)], axis=1).astype(BF16)


def local(
    context, stream, w_attn_out, modulation, w_teacher_head, noisy, timestep, frames,
    w_in, w_time, w_up, w_down, w_out,
):
    phase = (timestep.astype(F32) / STEPS + 0.008) / 1.008 * (math.pi / 2)
    scalars = jnp.stack([jnp.cos(phase)[0], jnp.sin(phase)[0], frames.astype(F32)[0]])
    features = time_features(timestep).astype(F32)
    info = jnp.concatenate(
        [jnp.broadcast_to(scalars[:, None], (3, 128)), features, jnp.zeros((4, 128), F32)], axis=0
    )
    target, grad, loss = call(
        context.reshape(8, 32, 512), w_attn_out.T, w_up, w_down.T, stream, modulation.reshape(3, 1, 4096), w_teacher_head,
        noisy.reshape(8, 32, 128), info, w_out, w_in, w_time,
    )
    return target.reshape(256, C), loss[0, 0], grad


def solution(mesh):
    in_specs = (
        P("dp", "tp"),
        P("dp", None),
        P("tp", "dp"),
        P("dp", None, None),
        P("dp", None),
        P("dp", None),
        P("dp"),
        P("dp"),
        P(),
        P(),
        P("dp", "tp"),
        P("tp", "dp"),
        P("dp", None),
    )
    out_specs = (P("dp", None), P(), P("dp", "tp"))
    return jax.shard_map(local, mesh=mesh, in_specs=in_specs, out_specs=out_specs, check_vma=False)
```

```python
import math

import jax
import jax.numpy as jnp
from jax import lax
from jax.experimental import pallas as pl
from jax.experimental.pallas import tpu as pltpu
from jax.sharding import PartitionSpec as P

C = 128
FREQ = 128
STEPS = 1000
LOSS_SCALE = 32768.0
EPS = 1e-06
F32 = jnp.float32
BF16 = jnp.bfloat16
MESH = pl.DeviceIdType.MESH
N_SEND = 520

COUNTS = dict(
    ctx=8, ag=128, ring=36, sib=32, sp=16, st=16, mod=16, head=4, nf=16, wo1=4, wo2=16, cnt=4,
    dnx=4, dny=4, dn2x=4, dn2y=4, un=32, tm=16, gp=16, lx=16, tg=8, lt=8, lz=4, g1=4, g2=4, g3=4, g4=16,
)
BASE = {}
N_RECV = 0
for _name, _count in COUNTS.items():
    BASE[_name] = N_RECV
    N_RECV += _count

XY = [(dx, dy) for dx in range(4) for dy in range(4) if dx or dy]


def dot_nt(a, b):
    return lax.dot_general(a, b, (((1,), (1,)), ((), ())), preferred_element_type=F32)


def dot_nn(a, b):
    return jnp.dot(a, b, preferred_element_type=F32)


def dot_tn(a, b):
    return lax.dot_general(a, b, (((0,), (0,)), ((), ())), preferred_element_type=F32)


def split_dot(a, b):
    high = a.astype(BF16)
    low = (a - high.astype(F32)).astype(BF16)
    return dot_nn(high, b) + dot_nn(low, b)


def body(
    ctx, wa, wu, wd, stream, mod, head, noisy, info, wo, win, wtime,
    tgt_out, grad_out, loss_out,
    ctxp, w4, s4, upw, dnw, sp, srecv, strb, modb, headb, nfb, woutb, wit, lifted, slope, hidden, dnsend,
    dnx, dny, sx, sy, dn2x, dn2y,
    unitb, ubuf, gbuf, att, zbuf, tsend, trecv, gpb, tgb, g1, r1, g2, r2, g3, r3, g4s, g4r,
    lx, lt, lz, cz, send_sem, recv_sem,
):
    tp = lax.axis_index("tp")
    dp = lax.axis_index("dp")
    zh, c = lax.div(tp, 2), lax.rem(tp, 2)
    xy, zl = lax.div(dp, 4), lax.rem(dp, 4)
    x, y = lax.div(xy, 4), lax.rem(xy, 4)
    z = zh * 4 + zl
    sibling = zh * 2 + (1 - c)

    def plane(dx, dy):
        return lax.rem(x + dx, 4) * 4 + lax.rem(y + dy, 4)

    def other(v, d):
        return lax.rem(v + d, 4)

    barrier = pltpu.get_barrier_semaphore()
    partners = [(tp, plane(dx, dy) * 4 + zl) for dx, dy in XY]
    partners += [(lax.rem(tp + d, 8), dp) for d in range(1, 8)]
    for step in (1, 15):
        zz = lax.rem(z + step, 16)
        partners.append((lax.div(zz, 4) * 2 + c, xy * 4 + lax.rem(zz, 4)))
    partners += [(tp, xy * 4 + other(zl, d)) for d in (1, 2, 3)]
    for p_tp, p_dp in partners:
        pl.semaphore_signal(barrier, inc=1, device_id={"tp": p_tp, "dp": p_dp}, device_id_type=MESH)
    pl.semaphore_wait(barrier, len(partners))

    sends = []

    def send(src, dst, kind, index, to_tp, to_dp):
        copy = pltpu.make_async_remote_copy(
            src_ref=src, dst_ref=dst,
            send_sem=send_sem.at[len(sends)], recv_sem=recv_sem.at[BASE[kind] + index],
            device_id={"tp": to_tp, "dp": to_dp}, device_id_type=MESH,
        )
        copy.start()
        sends.append(copy)

    def arrived(dst, kind, index):
        pltpu.make_async_remote_copy(
            src_ref=dst, dst_ref=dst,
            send_sem=send_sem.at[0], recv_sem=recv_sem.at[BASE[kind] + index],
            device_id={"tp": tp, "dp": dp}, device_id_type=MESH,
        ).wait_recv()

    def to_plane(source, target, kind):
        for dx, dy in XY:
            p = plane(dx, dy)
            send(source(p), target.at[xy], kind, xy, tp, p * 4 + zl)

    def from_plane(target, kind):
        for dx, dy in XY:
            p = plane(dx, dy)
            arrived(target.at[p], kind, p)

    def gather_own(view, kind, base):
        for d in (1, 3, 2):
            px, py = other(x, d) * 4 + y, x * 4 + other(y, d)
            send(view(xy, None), view(xy, None), kind, base + xy * 2, tp, px * 4 + zl)
            send(view(xy, None), view(xy, None), kind, base + xy * 2, tp, py * 4 + zl)

    def gather_forward(view, kind, base):
        for d in (1, 3, 2):
            px, py = other(x, d) * 4 + y, x * 4 + other(y, d)
            arrived(view(px, None), kind, base + px * 2)
            for e in (1, 3, 2):
                send(view(px, 0), view(px, 0), kind, base + px * 2, tp, (x * 4 + other(y, e)) * 4 + zl)
            arrived(view(py, None), kind, base + py * 2)
            for e in (1, 3, 2):
                send(view(py, 1), view(py, 1), kind, base + py * 2 + 1, tp, (other(x, e) * 4 + y) * 4 + zl)

    def gather_last(view, kind, base):
        for dx in (1, 2, 3):
            for dy in (1, 2, 3):
                p = plane(dx, dy)
                arrived(view(p, 0), kind, base + p * 2)
                arrived(view(p, 1), kind, base + p * 2 + 1)

    def ctx_view(chunk):
        def view(source, half):
            if half is None:
                return ctxp.at[pl.ds(2 * chunk, 2), source]
            return ctxp.at[pl.ds(2 * chunk, 2), source, pl.ds(16 * half, 16)]

        return view

    def unit_view(source, half):
        if half is None:
            return unitb.at[source]
        return unitb.at[source, pl.ds(16 * half, 16)]

    def slot(kind, zz, core):
        if kind == 0:
            return w4.at[lax.div(zz, 4) * 2 + core, lax.rem(zz, 4)]
        return s4.at[core, lax.div(zz, 4), lax.rem(zz, 4)]

    def ring_send(kind, zz, hop, direction):
        to = lax.rem(z + (1 if direction == 0 else 15), 16)
        ref = slot(kind, zz, c)
        send(ref, ref, "ring", (kind * 2 + direction) * 9 + hop,
             lax.div(to, 4) * 2 + c, xy * 4 + lax.rem(to, 4))

    def sibling_send(kind, zz):
        ref = slot(kind, zz, c)
        send(ref, ref, "sib", kind * 16 + zz, sibling, dp)

    def ring_start(kind):
        ring_send(kind, z, 1, 0)
        ring_send(kind, z, 1, 1)
        sibling_send(kind, z)

    def ring_step(kind, hop):
        for direction, last in ((0, 8), (1, 7)):
            if hop > last:
                continue
            zz = lax.rem(z + (16 - hop if direction == 0 else hop), 16)
            arrived(slot(kind, zz, c), "ring", (kind * 2 + direction) * 9 + hop)
            if hop < last:
                ring_send(kind, zz, hop + 1, direction)
            sibling_send(kind, zz)

    def ring_last(kind):
        for zz in range(16):
            arrived(slot(kind, zz, 1 - c), "sib", kind * 16 + zz)

    ctxp[tp, xy] = ctx[tp]
    for d in (1, 2, 7, 6, 3, 5, 4):
        t = lax.rem(tp + d, 8)
        send(ctx.at[t], ctxp.at[tp, xy], "ctx", tp, t, dp)
    selects = [select_units(q) for q in range(3)]
    unused = [jnp.zeros((128, 32), F32)]
    up = [dot_nt(selects[q], wu[...]) for q in range(3)] + unused
    down = [dot_nt(selects[q], wd[...]) for q in range(3)] + unused
    sp[:, 0:8] = jnp.concatenate(up, axis=1).reshape(16, 8, 128).astype(BF16)
    sp[:, 8:16] = jnp.concatenate(down, axis=1).reshape(16, 8, 128).astype(BF16)
    srecv[xy] = sp[xy]
    to_plane(lambda p: sp.at[p], srecv, "sp")
    nfb[xy, 0:32, 0:128] = noisy[tp]
    nfb[xy, 0:32, 128:256] = jnp.broadcast_to(info[3:4], (32, 128)).astype(BF16)
    nfb[xy, 32:48, 0:128] = jnp.broadcast_to(info[2:3], (16, 128)).astype(BF16)
    nfb[xy, 32:48, 128:256] = jnp.zeros((16, 128), BF16)
    to_plane(lambda p: nfb.at[xy], nfb, "nf")
    w4[tp, zl] = wa[...]
    ring_start(0)
    woutb[zl, xy] = wo[...]
    headb[zl] = head[...]
    for d in (1, 2, 3):
        other_dp = xy * 4 + other(zl, d)
        send(wo, woutb.at[zl, xy], "wo1", zl, tp, other_dp)
        send(head, headb.at[zl], "head", zl, tp, other_dp)
    rows = pl.ds(pl.multiple_of(tp * 32, 32), 32)
    own_stream = pltpu.make_async_copy(
        stream.at[rows, pl.ds(pl.multiple_of(xy * 256, 256), 256)], strb.at[xy], send_sem.at[N_SEND - 1]
    )
    own_stream.start()

    def small_sends():
        modb[xy] = mod[:, :, pl.ds(pl.multiple_of(xy * 256, 256), 256)]
        to_plane(lambda p: mod.at[:, :, pl.ds(pl.multiple_of(p * 256, 256), 256)], modb, "mod")
        to_plane(lambda p: stream.at[rows, pl.ds(pl.multiple_of(p * 256, 256), 256)], strb, "st")

    def ctx_own(chunk_step):
        chunk = other(zh, chunk_step)
        if chunk_step == 0:
            arrived(ctxp.at[sibling, xy], "ctx", sibling)
        else:
            arrived(ctxp.at[2 * chunk, xy], "ctx", 2 * chunk)
            arrived(ctxp.at[2 * chunk + 1, xy], "ctx", 2 * chunk + 1)
        gather_own(ctx_view(chunk), "ag", chunk * 32)

    def ctx_forward(chunk_step):
        chunk = other(zh, chunk_step)
        gather_forward(ctx_view(chunk), "ag", chunk * 32)

    group = lax.div(lax.broadcasted_iota(jnp.int32, (16, 128), 1), 32)
    from_plane(srecv, "sp")
    for t in range(4):
        pieces = [srecv[4 * t + g].astype(F32) for g in range(4)]
        for q in range(3):
            tile = jnp.zeros((16, 128), F32)
            for g in range(4):
                shift = ((g - q) * 32) % 128
                moved = pltpu.roll(pieces[g], shift, 1) if shift else pieces[g]
                tile = jnp.where(group == g, moved, tile)
            hidden[8 * q : 8 * q + 8, 128 * t : 128 * t + 128] = tile[0:8]
            hidden[24 + 8 * q : 32 + 8 * q, 128 * t : 128 * t + 128] = tile[8:16]
    s4[c, zh, zl] = hidden[0:48, 0:512].astype(BF16)
    ring_start(1)

    ctx_own(0)

    def lift(block):
        piece = nfb[4 * block : 4 * block + 4, 0:32].reshape(128, 256)
        for n in range(4):
            v = dot_nn(piece, wit[:, 512 * n : 512 * n + 512])
            v = v / (1.0 + jnp.exp(-v))
            lifted[128 * block : 128 * block + 128, 512 * n : 512 * n + 512] = v.astype(BF16)

    group128 = lax.div(lax.broadcasted_iota(jnp.int32, (128, 128), 1), 32)

    def order_features(zo):
        for half, source in ((0, win), (1, wtime)):
            for t in range(4):
                tile = jnp.zeros((128, 128), F32)
                for g in range(4):
                    piece = source[:, 128 * (4 * t + g) : 128 * (4 * t + g) + 128].astype(F32)
                    shift = ((g - zo) * 32) % 128
                    moved = pltpu.roll(piece, shift, 1) if shift else piece
                    tile = jnp.where(group128 == g, moved, tile)
                at = 512 * zo + 128 * t
                wit[128 * half : 128 * half + 128, at : at + 128] = tile.astype(BF16)

    k0 = math.sqrt(2.0 / math.pi)

    def up_part(zb):
        return upw[:, 512 * zb : 512 * zb + 512]

    def down_part(zb):
        return dnw[:, 512 * zb : 512 * zb + 512]

    def student(block):
        rs = slice(256 * block, 256 * block + 256)
        pre = dot_nt(lifted[rs, 0:512], up_part(0))
        for zb in range(1, 4):
            pre = pre + dot_nt(lifted[rs, 512 * zb : 512 * zb + 512], up_part(zb))
        tangent = jnp.tanh(k0 * (pre + 0.044715 * pre * pre * pre))
        slope[rs] = 0.5 * (1.0 + tangent) + 0.5 * pre * (1.0 - tangent * tangent) * k0 * (
            1.0 + 3.0 * 0.044715 * pre * pre
        )
        act = (0.5 * pre * (1.0 + tangent)).astype(BF16)
        for zb in range(4):
            part = dot_nn(act, down_part(zb)).astype(BF16)
            dnsend[2 * block : 2 * block + 2, :, :, 512 * zb : 512 * zb + 512] = part.reshape(2, 4, 32, 512)

    def share_out():
        for d in (1, 2, 3):
            zo = other(zl, d)
            arrived(woutb.at[zo, xy], "wo1", zo)
        for dx, dy in XY:
            p = plane(dx, dy)
            send(woutb.at[:, xy], woutb.at[:, xy], "wo2", xy, tp, p * 4 + zl)

    def share_count():
        count_part = nfb[0, 32:40, 0:128].astype(F32)
        for s in range(1, 16):
            count_part = count_part + nfb[s, 32:40, 0:128].astype(F32)
        cz[zl] = count_part
        for d in (1, 2, 3):
            send(cz.at[zl], cz.at[zl], "cnt", zl, tp, xy * 4 + other(zl, d))

    small_sends()
    order_features(0)
    ring_step(1, 1)
    ring_step(0, 1)
    ctx_own(1)
    order_features(1)
    ring_step(1, 2)
    ring_step(0, 2)
    ctx_own(3)
    order_features(2)
    order_features(3)
    ring_step(1, 3)
    ring_step(0, 3)
    share_out()
    ctx_own(2)
    from_plane(nfb, "nf")
    ctx_forward(0)
    ring_step(1, 4)
    ring_step(0, 4)
    lift(0)
    lift(1)
    ctx_forward(1)
    ring_step(1, 5)
    ring_step(0, 5)
    lift(2)
    lift(3)
    ring_step(1, 6)
    ring_step(0, 6)
    ctx_forward(3)
    share_count()
    ring_step(1, 7)
    ring_step(0, 7)
    ctx_forward(2)
    ring_step(1, 8)
    ring_step(0, 8)
    ring_last(1)
    for zb in range(4):
        whole = s4[:, :, zb].astype(F32)
        upw[:, 512 * zb : 512 * zb + 512] = whole[:, :, 0:24].reshape(192, 512).astype(BF16)
        dnw[:, 512 * zb : 512 * zb + 512] = whole[:, :, 24:48].reshape(192, 512).astype(BF16)
    student(0)
    student(1)
    for d in (1, 3, 2):
        xo, yo = other(x, d), other(y, d)
        send(dnsend.at[xo, :, :, pl.ds(0, 1024)], dnx.at[x], "dnx", x, tp, (xo * 4 + y) * 4 + zl)
        send(dnsend.at[:, yo, :, pl.ds(1024, 1024)], dny.at[y], "dny", y, tp, (x * 4 + yo) * 4 + zl)
    dnx[x] = dnsend[x, :, :, 0:1024]
    dny[y] = dnsend[:, y, :, 1024:2048]
    ring_last(0)
    for d in (1, 3, 2):
        xo, yo = other(x, d), other(y, d)
        arrived(dnx.at[xo], "dnx", xo)
        arrived(dny.at[yo], "dny", yo)
    for k in range(4):
        sx[k] = sum(dnx[o, k].astype(F32) for o in range(4)).astype(BF16)
        sy[k] = sum(dny[o, k].astype(F32) for o in range(4)).astype(BF16)
    dn2x[y] = sx[y]
    dn2y[x] = sy[x]
    for d in (1, 3, 2):
        xo, yo = other(x, d), other(y, d)
        send(sx.at[yo], dn2x.at[y], "dn2x", y, tp, (x * 4 + yo) * 4 + zl)
        send(sy.at[xo], dn2y.at[x], "dn2y", x, tp, (xo * 4 + y) * 4 + zl)

    for d in (1, 2, 3):
        zo = other(zl, d)
        arrived(headb.at[zo], "head", zo)
    for step in (0, 1, 3, 2):
        gather_last(ctx_view(other(zh, step)), "ag", other(zh, step) * 32)
    att[...] = jnp.zeros_like(att)

    def att_step(t, carry):
        att[...] += dot_nt(ctxp[t].reshape(512, 512), w4[t].reshape(256, 512))
        return carry

    lax.fori_loop(0, 8, att_step, 0)

    from_plane(_Columns(woutb), "wo2")
    whole_out = woutb[...].reshape(2048, 128)
    fold = dot_nn(down_part(0), whole_out[0:512])
    for zb in range(1, 4):
        fold = fold + dot_nn(down_part(zb), whole_out[512 * zb : 512 * zb + 512])
    gbuf[...] = fold.astype(BF16)
    own_nf = nfb[xy, 0:32]
    mixed = dot_nn(own_nf, wit[...])
    for d in (1, 3, 2):
        xo, yo = other(x, d), other(y, d)
        arrived(dn2x.at[yo], "dn2x", yo)
        arrived(dn2y.at[xo], "dn2y", xo)
    down_x = sum(dn2x[o].astype(F32) for o in range(4))
    down_y = sum(dn2y[o].astype(F32) for o in range(4))
    mixed = mixed + jnp.concatenate([down_x, down_y], axis=1)
    inv_rms = lax.rsqrt(jnp.mean(mixed * mixed, axis=-1, keepdims=True) + EPS)
    unit_b = (mixed * inv_rms).astype(BF16)
    unitb[xy] = unit_b
    gather_own(unit_view, "un", 0)
    pred = dot_nn(unit_b, whole_out)

    from_plane(strb, "st")
    from_plane(modb, "mod")
    own_stream.wait()
    lane = lax.broadcasted_iota(jnp.int32, (32, 128), 1)

    def norm_step(s, carry):
        state = strb[s].astype(F32) + modb[s, 0] * att[pl.ds(pl.multiple_of(s * 32, 32), 32)]
        center = jnp.mean(state, axis=-1, keepdims=True)
        state = state - center
        square = jnp.sum(state * state, axis=-1, keepdims=True)
        zbuf[s] = (state * (1.0 + modb[s, 2])).astype(BF16)
        tsend[s, 32:64] = jnp.where(lane < 64, center, square)
        return carry

    lax.fori_loop(0, 16, norm_step, 0)
    whole_head = headb[...].reshape(256, 128)
    tsend[:, 0:32] = dot_nn(zbuf[...].reshape(512, 256), whole_head).reshape(16, 32, 128)
    vectors = jnp.concatenate([modb[:, 1, 0], 1.0 + modb[:, 2, 0]], axis=0)
    vectors = split_dot(vectors, whole_head)
    tsend[:, 65] = vectors[0:16]
    tsend[:, 66] = vectors[16:32]
    trecv[xy] = tsend[xy]
    to_plane(lambda p: tsend.at[p], trecv, "tm")
    gather_forward(unit_view, "un", 0)


    for d in (1, 2, 3):
        zo = other(zl, d)
        arrived(cz.at[zo], "cnt", zo)
    count = cz[0, 0:1] + cz[1, 0:1] + cz[2, 0:1] + cz[3, 0:1]
    from_plane(trecv, "tm")
    velocity = trecv[0, 0:32]
    center = trecv[0, 32:64, 0:1]
    square = trecv[0, 32:64, 127:128]
    shift_row = trecv[0, 65:66]
    for s in range(1, 16):
        velocity = velocity + trecv[s, 0:32]
        center = center + trecv[s, 32:64, 0:1]
        square = square + trecv[s, 32:64, 127:128]
        shift_row = shift_row + trecv[s, 65:66]
    center = center * (1.0 / 16.0)
    for s in range(16):
        gap = trecv[s, 32:64, 0:1] - center
        square = square + 256.0 * gap * gap
        velocity = velocity + gap * trecv[s, 66:67]
    velocity = velocity * lax.rsqrt(square * (1.0 / 4096.0) + EPS) + shift_row
    target = info[0:1] * velocity + info[1:2] * own_nf[:, 0:128].astype(F32)
    tgb[tp] = target
    frame = (lax.broadcasted_iota(jnp.int32, (32, 128), 0) + tp * 32).astype(F32)
    live = (frame < info[2:3]).astype(F32)
    error = pred - target
    grad_pred = (LOSS_SCALE * 2.0 / (count * C)) * live * error
    along = jnp.sum(grad_pred * pred, axis=-1, keepdims=True) * (1.0 / 2048.0)
    gpb[xy, :, 0:128] = (inv_rms * grad_pred).astype(BF16)
    gpb[xy, :, 128:256] = jnp.broadcast_to(inv_rms * along, (32, 128)).astype(BF16)
    to_plane(lambda p: gpb.at[xy], gpb, "gp")
    lx[xy] = jnp.broadcast_to(jnp.sum(live * error * error), (8, 128))
    to_plane(lambda p: lx.at[xy], lx, "lx")
    for d in (1, 2, 7, 6, 3, 5, 4):
        send(tgb.at[tp], tgb.at[tp], "tg", tp, lax.rem(tp + d, 8), dp)

    gather_last(unit_view, "un", 0)
    for block in range(4):
        piece = unitb[4 * block : 4 * block + 4].reshape(128, 2048)
        along_down = dot_nt(piece[:, 0:512], down_part(0))
        for zb in range(1, 4):
            along_down = along_down + dot_nt(piece[:, 512 * zb : 512 * zb + 512], down_part(zb))
        ubuf[128 * block : 128 * block + 128] = along_down
    from_plane(gpb, "gp")
    both = gpb[...].reshape(512, 256)
    grad_hidden = dot_nt(both[:, 0:128], gbuf[...]) - both[:, 128:129].astype(F32) * ubuf[...]
    grad_pre = (grad_hidden * slope[...]).astype(BF16)

    def both_cores(zb):
        arrived(r1.at[zb], "g1", zb)
        g2[zb] = (g1[zb, c] + r1[zb]).reshape(96, 512).astype(BF16)
        if zb is not zl:
            send(g2.at[zb], r2.at[zl], "g2", zl, tp, xy * 4 + zb)

    previous = None
    for d in (2, 1, 3, 0):
        zb = other(zl, d) if d else zl
        columns = pl.ds(pl.multiple_of(zb * 512, 512), 512)
        g1[zb] = dot_tn(grad_pre, lifted[:, columns]).reshape(2, 4, 24, 512)
        send(g1.at[zb, 1 - c], r1.at[zb], "g1", zb, sibling, dp)
        if previous is not None:
            both_cores(previous)
        previous = zb
    both_cores(zl)
    r2[zl] = g2[zl]
    from_plane(lx, "lx")
    loss_sum = lx[0]
    for s in range(1, 16):
        loss_sum = loss_sum + lx[s]
    lt[tp] = loss_sum
    for d in range(1, 8):
        send(lt.at[tp], lt.at[tp], "lt", tp, lax.rem(tp + d, 8), dp)
    for d in (1, 2, 3):
        zo = other(zl, d)
        arrived(r2.at[zo], "g2", zo)
    part = r2[0].astype(F32) + r2[1].astype(F32) + r2[2].astype(F32) + r2[3].astype(F32)
    part = jnp.concatenate([part.reshape(4, 24, 512), jnp.zeros((4, 8, 512), F32)], axis=1)
    g3[...] = part.astype(BF16)
    r3[zh] = g3[zh]
    for d in (1, 2, 3):
        ho = other(zh, d)
        send(g3.at[ho], r3.at[zh], "g3", zh, ho * 2 + c, dp)
    for d in range(1, 8):
        t = lax.rem(tp + d, 8)
        arrived(lt.at[t], "lt", t)
    loss_sum = lt[0]
    for s in range(1, 8):
        loss_sum = loss_sum + lt[s]
    lz[zl] = loss_sum
    for d in (1, 2, 3):
        send(lz.at[zl], lz.at[zl], "lz", zl, tp, xy * 4 + other(zl, d))
    for d in (1, 2, 3):
        ho = other(zh, d)
        arrived(r3.at[ho], "g3", ho)
    total = r3[0].astype(F32) + r3[1].astype(F32) + r3[2].astype(F32) + r3[3].astype(F32)
    group8 = lax.div(lax.broadcasted_iota(jnp.int32, (8, 128), 1), 32)
    for t in range(4):
        for g in range(4):
            tile = jnp.zeros((8, 128), F32)
            for q in range(3):
                shift = ((q - g) * 32) % 128
                piece = total[8 * q : 8 * q + 8, 128 * t : 128 * t + 128]
                moved = pltpu.roll(piece, shift, 1) if shift else piece
                tile = jnp.where(group8 == q, moved, tile)
            g4s[4 * t + g] = tile
    g4r[xy] = g4s[xy]
    to_plane(lambda p: g4s.at[p], g4r, "g4")
    for d in (1, 2, 3):
        zo = other(zl, d)
        arrived(lz.at[zo], "lz", zo)
    loss_out[...] = (lz[0] + lz[1] + lz[2] + lz[3]) / (count * C)
    for d in range(1, 8):
        t = lax.rem(tp + d, 8)
        arrived(tgb.at[t], "tg", t)
    tgt_out[...] = tgb[...]
    from_plane(g4r, "g4")
    part = g4r[...].reshape(128, 128)
    high = part.astype(BF16)
    part = part - high.astype(F32)
    middle = part.astype(BF16)
    low = (part - middle.astype(F32)).astype(BF16)
    grad = jnp.zeros((32, 384), F32)
    for q in range(3):
        chosen = dot_tn(high, selects[q]) + dot_tn(middle, selects[q]) + dot_tn(low, selects[q])
        grad = grad + chosen[32 * q : 32 * q + 32]
    grad_out[...] = grad
    for copy in sends:
        copy.wait_send()
    assert len(sends) < N_SEND


def select_units(q):
    row = lax.broadcasted_iota(jnp.int32, (128, 384), 0)
    unit = lax.broadcasted_iota(jnp.int32, (128, 384), 1)
    r = lax.rem(row, 8)
    chosen = unit == lax.div(row, 8) * 24 + q * 8 + r
    return jnp.where(chosen, 1.0, 0.0).astype(BF16)


class _Columns:
    def __init__(self, ref):
        self.ref = ref

    @property
    def at(self):
        return self

    def __getitem__(self, p):
        return self.ref.at[:, p]


def call(*args):
    vmem = pl.BlockSpec(memory_space=pltpu.VMEM)
    hbm = pl.BlockSpec(memory_space=pl.ANY)
    V = pltpu.VMEM
    return pl.pallas_call(
        body,
        out_shape=(
            jax.ShapeDtypeStruct((8, 32, 128), F32),
            jax.ShapeDtypeStruct((32, 384), F32),
            jax.ShapeDtypeStruct((8, 128), F32),
        ),
        in_specs=[vmem] * 4 + [hbm] + [vmem] * 7,
        out_specs=(vmem, vmem, vmem),
        scratch_shapes=[
            V((8, 16, 32, 512), BF16),
            V((8, 4, 64, 512), BF16),
            V((2, 4, 4, 48, 512), BF16),
            V((192, 2048), BF16),
            V((192, 2048), BF16),
            V((16, 16, 128), BF16),
            V((16, 16, 128), BF16),
            V((16, 32, 256), BF16),
            V((16, 3, 1, 256), F32),
            V((4, 64, 128), BF16),
            V((16, 48, 256), BF16),
            V((4, 16, 32, 128), BF16),
            V((256, 2048), BF16),
            V((512, 2048), BF16),
            V((512, 192), F32),
            V((64, 512), F32),
            V((4, 4, 32, 2048), BF16),
            V((4, 4, 32, 1024), BF16),
            V((4, 4, 32, 1024), BF16),
            V((4, 32, 1024), BF16),
            V((4, 32, 1024), BF16),
            V((4, 32, 1024), BF16),
            V((4, 32, 1024), BF16),
            V((16, 32, 2048), BF16),
            V((512, 192), F32),
            V((192, 128), BF16),
            V((512, 256), F32),
            V((16, 32, 256), BF16),
            V((16, 72, 128), F32),
            V((16, 72, 128), F32),
            V((16, 32, 256), BF16),
            V((8, 32, 128), F32),
            V((4, 2, 4, 24, 512), F32),
            V((4, 4, 24, 512), F32),
            V((4, 96, 512), BF16),
            V((4, 96, 512), BF16),
            V((4, 32, 512), BF16),
            V((4, 32, 512), BF16),
            V((16, 8, 128), F32),
            V((16, 8, 128), F32),
            V((16, 8, 128), F32),
            V((8, 8, 128), F32),
            V((4, 8, 128), F32),
            V((4, 8, 128), F32),
            pltpu.SemaphoreType.DMA((N_SEND,)),
            pltpu.SemaphoreType.DMA((N_RECV,)),
        ],
        compiler_params=pltpu.CompilerParams(
            collective_id=0, has_side_effects=True, vmem_limit_bytes=56 * 1024 * 1024
        ),
    )(*args)


def time_features(timestep):
    half = FREQ // 2
    freq_index = jnp.arange(half, dtype=F32)
    rates = jnp.exp(-math.log(10000.0) * freq_index / half)
    angles = timestep.astype(F32)[:, None] * rates[None, :]
    return jnp.concatenate([jnp.sin(angles), jnp.cos(angles)], axis=1).astype(BF16)


def local(
    context, stream, w_attn_out, modulation, w_teacher_head, noisy, timestep, frames,
    w_in, w_time, w_up, w_down, w_out,
):
    phase = (timestep.astype(F32) / STEPS + 0.008) / 1.008 * (math.pi / 2)
    scalars = jnp.stack([jnp.cos(phase)[0], jnp.sin(phase)[0], frames.astype(F32)[0]])
    features = time_features(timestep).astype(F32)
    info = jnp.concatenate(
        [jnp.broadcast_to(scalars[:, None], (3, 128)), features, jnp.zeros((4, 128), F32)], axis=0
    )
    target, grad, loss = call(
        context.reshape(8, 32, 512), w_attn_out.T, w_up, w_down.T, stream, modulation.reshape(3, 1, 4096), w_teacher_head,
        noisy.reshape(8, 32, 128), info, w_out, w_in, w_time,
    )
    return target.reshape(256, C), loss[0, 0], grad


def solution(mesh):
    in_specs = (
        P("dp", "tp"),
        P("dp", None),
        P("tp", "dp"),
        P("dp", None, None),
        P("dp", None),
        P("dp", None),
        P("dp"),
        P("dp"),
        P(),
        P(),
        P("dp", "tp"),
        P("tp", "dp"),
        P("dp", None),
    )
    out_specs = (P("dp", None), P(), P("dp", "tp"))
    return jax.shard_map(local, mesh=mesh, in_specs=in_specs, out_specs=out_specs, check_vma=False)
```
